128 devices in a mesh: gx: 16 (over y, x), gy: 8 (over z, core).
Axes of the slice: x: 4, y: 4, z: 4, core: 2. Of those that a mesh axis runs over, the one named last changes fastest.
Arguments:
- atm_state: float32 [6, 786432], P(None, ('gx', 'gy')), may hold values from -6 to 6
- pair_block: int32 [32768], P(('gx', 'gy')), may hold values from 0 to 47
- pair_owner: int32 [32768, 1], P(('gx', 'gy')), may hold values from 0 to 127; in each aligned block of 256 rows (0 to 255, 256 to 511, ...) at most 4 rows name the same one
- pair_row: int32 [32768], P(('gx', 'gy')), may hold values from 0 to 63
- pair_tile: int32 [32768], P(('gx', 'gy')), may hold values from 0 to 127
- remap_weight: bfloat16 [16384, 128, 128], P(('gx', 'gy')), may hold values from 0.0014953613 to 0.029907227
- wet_mask: int32 [1024, 1024], P('gx', 'gy'), may hold values 0 or 1
- ocean_state: float32 [4, 16, 1024, 1024], P(None, None, 'gx', 'gy'), may hold values from -6 to 6
- vert_kappa: float32 [16, 1024, 1024], P(None, 'gx', 'gy'), may hold values from 0.05 to 3
- horiz_kappa: float32 [1024, 1024], P('gx', 'gy'), may hold values from 0.02 to 0.24
Outputs:
- ocean_next: float32 [4, 16, 1024, 1024], P(None, None, 'gx', 'gy')
- atm_surface: float32 [4, 786432], P(None, ('gx', 'gy'))
The draws below stay inside these ranges and needn't reach their ends.
Inputs may be any that keep to these rules, and one draw needn't show every extreme that they name: `pair_owner`: the intersections of one device name one owner at most 4 times, and exactly 4 times for some owner.
All inputs are finite; a program needn't handle non-finite values. No bound on the sum of `wet_mask` on one device may be relied on, other than what follows from the above.
Results may differ from the reference program's by a relative error of at most 0.0039.
Values sent between devices are 32-bit elements; how exact they have to be, the bound alone decides.
A program may use at most 64 MiB of HBM per device.

```python
import math
import jax
import jax.numpy as jnp
import numpy as np
from jax import lax

TX = 64
TY = 128
LEV = 16
ABLK = 128
NBLK_DEV = 48
NPAIR = 256
NTILE = 128
CAP = 4
NXO = 1024
NYO = 1024
ATM_COLS = 786432
N_GX = 16
N_GY = 8
DEVICES = 128


def place_ends(values, rng, smallest, high):
    dims = values.shape
    spot = [jax.random.randint(jax.random.fold_in(rng, axis), (), 0, dims[axis]) for axis in range(len(dims))]
    values = values.at[tuple(spot)].set(smallest)
    longest = dims.index(max(dims))
    spot[longest] = (spot[longest] + 1) % dims[longest]
    return values.at[tuple(spot)].set(high)


def steps_of(stream_key, extent, split, least, high):
    def one(axis_at, shards_of):
        heights = jax.random.uniform(jax.random.fold_in(jax.random.fold_in(stream_key, 6), axis_at), (shards_of,), jnp.float32, least / len(split), high / len(split))
        return jnp.repeat(jnp.exp(heights), extent[axis_at] // shards_of).reshape((-1,) + (1,) * (len(extent) - axis_at - 1))

    level = one(*split[0])
    for cut in split[1:]:
        level = level * one(*cut)
    return level


def assign_block(key, own, number, rows, count, top, limit, slope):
    sequence = jax.random.permutation(key, count)
    crowded, usual = load_shares(count, rows * top, limit, slope, True), load_shares(count, rows * top, limit, slope, False)
    places = jnp.arange(count)

    def named(sizes, offset_by):
        used = int((sizes > 0).sum())
        fixed = max(1, used // 4)
        moved = fixed + (places - fixed + offset_by * (used - fixed)) % max(1, count - fixed)
        return jnp.zeros((count,), jnp.int32).at[sequence[jnp.where(places < fixed, places, moved)]].set(jnp.asarray(sizes, jnp.int32))

    sizes = jnp.where(number % 4 == 0, named(crowded, number // 4), named(usual, number - number // 4 - 1))
    mixed = jax.random.permutation(jax.random.fold_in(own, 3), count)
    giver, receiver = mixed[0:count // 2 * 2:2], mixed[1:count // 2 * 2:2]
    margin = jnp.minimum(sizes[giver] - 1, limit - sizes[receiver]) // 2
    margin = jnp.where((giver == sequence[0]) | (receiver == sequence[0]) | (sizes[receiver] == 0), 0, jnp.maximum(margin, 0))
    moved = jax.random.randint(jax.random.fold_in(own, 4), (count // 2,), 0, 1 << 20) % (margin + 1)
    sizes = sizes.at[giver].add(-moved).at[receiver].add(moved)
    labels = jnp.searchsorted(jnp.cumsum(sizes), jnp.arange(rows * top), side="right").astype(jnp.int32)
    table = labels.reshape(top, rows).T
    table = table[jax.random.permutation(jax.random.fold_in(own, 1), rows)]
    offset_by = jax.random.randint(jax.random.fold_in(own, 2), (rows, 1), 0, top)
    return jnp.take_along_axis(table, (jnp.arange(top)[None, :] + offset_by) % top, axis=1)


def load_shares(count, total, most, skew, full):
    loads = [(1 << 20) // math.isqrt(grade ** skew) + 1 for grade in range(1, count + 1)]
    largest = most if full else min(most, max(-(-total // count), total * loads[0] // sum(loads)))
    least = 1 if total - largest >= count - 1 else 0
    counts, surplus = [largest] + [least] * (count - 1), total - largest - least * (count - 1)
    while surplus > 0:
        candidates = [i for i in range(1, count) if counts[i] < largest] or [i for i in range(1, count) if counts[i] < most]
        whole, remaining = sum([loads[i] for i in candidates]), surplus
        for i in candidates:
            addition = min(most - counts[i], max(1, remaining * loads[i] // whole), surplus)
            counts[i] = counts[i] + addition
            surplus = surplus - addition
    return np.array(counts)


def normal_values(rng, dims, spread, reach, shards=(), kind=jnp.bfloat16):
    values = jax.random.normal(rng, dims, jnp.float32) * spread
    if len(shards) > 0:
        values = steps_of(rng, dims, shards, -0.22, 0.18) * values
    return jnp.clip(values, min=-reach, max=reach).astype(kind)


def setup_inputs(seed: int = 0) -> dict:
    key_list = jax.random.split(jax.random.key(seed), 11)
    atm_state = normal_values(key_list[0], (6, ATM_COLS), 1.0, 6.0, ((1, 128),), jnp.float32)
    pair_block = place_ends(jax.random.randint(key_list[1], (DEVICES * NPAIR,), 0, NBLK_DEV), jax.random.fold_in(key_list[1], 1), 0, NBLK_DEV - 1).astype(jnp.int32)
    pair_owner_keys = jax.random.split(jax.random.fold_in(key_list[2], 1), (DEVICES * NPAIR) // NPAIR)
    pair_owner_turns = jax.random.permutation(jax.random.fold_in(key_list[2], 3), (DEVICES * NPAIR) // NPAIR)
    pair_owner = jax.vmap(lambda own, number: assign_block(jax.random.fold_in(key_list[2], 2), own, number, NPAIR, DEVICES, 1, CAP, 2))(pair_owner_keys, pair_owner_turns).reshape((DEVICES * NPAIR, 1))
    pair_row = place_ends(jax.random.randint(key_list[3], (DEVICES * NPAIR,), 0, TX), jax.random.fold_in(key_list[3], 1), 0, TX - 1).astype(jnp.int32)
    pair_tile = place_ends(jax.random.randint(key_list[4], (DEVICES * NPAIR,), 0, NTILE), jax.random.fold_in(key_list[4], 1), 0, NTILE - 1).astype(jnp.int32)
    remap_weight = jnp.clip(jnp.exp(math.log(0.029907227) - 2.9957323 * jax.random.uniform(key_list[5], (DEVICES * NTILE, ABLK, TY), jnp.float32) ** steps_of(key_list[5], (DEVICES * NTILE, ABLK, TY), ((0, 128),), -0.2, 0.2)), 0.0014953613, 0.029907227).astype(jnp.bfloat16)
    wet_mask = place_ends((jax.random.randint(key_list[6], (NXO, NYO), 0, 10) < 7).astype(jnp.int32), jax.random.fold_in(key_list[6], 1), 0, 1)
    ocean_state = normal_values(key_list[7], (4, LEV, NXO, NYO), 1.0, 6.0, ((2, 16), (3, 8)), jnp.float32)
    vert_kappa = jnp.clip(jnp.exp(math.log(3.0) - 4.0943445 * jax.random.uniform(key_list[8], (LEV, NXO, NYO), jnp.float32) ** steps_of(key_list[8], (LEV, NXO, NYO), ((1, 16), (2, 8)), -0.2, 0.2)), 0.05, 3.0)
    horiz_kappa = jnp.clip(jnp.exp(math.log(0.24) - 2.4849066 * jax.random.uniform(key_list[9], (NXO, NYO), jnp.float32) ** steps_of(key_list[9], (NXO, NYO), ((0, 16), (1, 8)), -0.2, 0.2)), 0.02, 0.24)
    return dict(atm_state=atm_state, pair_block=pair_block, pair_owner=pair_owner, pair_row=pair_row, pair_tile=pair_tile, remap_weight=remap_weight, wet_mask=wet_mask, ocean_state=ocean_state, vert_kappa=vert_kappa, horiz_kappa=horiz_kappa)


def surface_flux(atm_state):
    wind_u = atm_state[0]
    wind_v = atm_state[1]
    speed = jnp.sqrt(wind_u * wind_u + wind_v * wind_v + 0.25)
    heat_flux = 0.5 * speed * (atm_state[2] - atm_state[5])
    water_flux = atm_state[4] - 0.3 * speed * atm_state[3]
    return jnp.stack([heat_flux, water_flux, 0.2 * speed * wind_u, 0.2 * speed * wind_v]).astype(jnp.bfloat16)

def column_mix(fields, vert_kappa):
    levels = vert_kappa.shape[0]
    face_coef = 0.5 * (vert_kappa[:-1] + vert_kappa[1:])
    zero_plane = jnp.zeros_like(vert_kappa[:1])
    above = jnp.concatenate([zero_plane, face_coef], 0)
    below = jnp.concatenate([face_coef, zero_plane], 0)
    diagonal = 1.0 + above + below
    upper_list = []
    rhs_list = []
    for level_index in range(levels):
        if level_index == 0:
            pivot_inv = 1.0 / diagonal[0]
            rhs_now = fields[:, 0] * pivot_inv
        else:
            pivot_inv = 1.0 / (diagonal[level_index] + above[level_index] * upper_list[-1])
            rhs_now = (fields[:, level_index] + above[level_index] * rhs_list[-1]) * pivot_inv
        upper_list.append(-below[level_index] * pivot_inv)
        rhs_list.append(rhs_now)
    solved = [rhs_list[-1]]
    for level_index in range(levels - 2, -1, -1):
        solved.append(rhs_list[level_index] - upper_list[level_index] * solved[-1])
    return jnp.stack(solved[::-1], 1)

def shifted(array, step_x, step_y):
    size_x = array.shape[-2]
    size_y = array.shape[-1]
    return array[..., 1 + step_x:size_x - 1 + step_x, 1 + step_y:size_y - 1 + step_y]

def diffuse(padded, coefficients):
    kappa_pad = coefficients[0]
    wet_pad = coefficients[1]
    centre = shifted(padded, 0, 0)
    kappa_mid = shifted(kappa_pad, 0, 0)
    wet_mid = shifted(wet_pad, 0, 0)
    result = centre
    for step_x, step_y in ((1, 0), (-1, 0), (0, 1), (0, -1)):
        face_coef = 0.25 * (kappa_mid + shifted(kappa_pad, step_x, step_y)) * wet_mid * shifted(wet_pad, step_x, step_y)
        result = result + face_coef * (shifted(padded, step_x, step_y) - centre)
    return result

def reference(atm_state, pair_block, pair_owner, pair_row, pair_tile, remap_weight, wet_mask, ocean_state, vert_kappa, horiz_kappa):
    highest = lax.Precision.HIGHEST
    devices = N_GX * N_GY
    fluxes = surface_flux(atm_state)
    blocks_all = fluxes.reshape(4, devices, NBLK_DEV, ABLK).transpose(1, 2, 0, 3)
    blocks_of = pair_block.reshape(devices, NPAIR)
    tiles_of = pair_tile.reshape(devices, NPAIR)
    weights_all = remap_weight.reshape(devices, NTILE, ABLK, TY)

    def forward_one(inputs):
        device_blocks, block_ids, tile_ids, device_weights = inputs
        picked = device_blocks[block_ids].astype(jnp.float32)
        chosen = device_weights[tile_ids].astype(jnp.float32)
        return jnp.einsum('pca,pab->pcb', picked, chosen, precision=highest)
    contrib = lax.map(forward_one, (blocks_all, blocks_of, tiles_of, weights_all)).reshape(devices * NPAIR, 4, TY)
    owner_ids = pair_owner[:, 0]
    cell_x = owner_ids // N_GY * TX + pair_row
    cell_g = owner_ids % N_GY
    forcing = jnp.zeros((NXO, N_GY, 4, TY), jnp.float32).at[cell_x, cell_g].add(contrib)
    forcing = forcing.transpose(2, 0, 1, 3).reshape(4, NXO, NYO)
    wet_frac = wet_mask.astype(jnp.float32)
    forced = ocean_state.at[:, 0].add(forcing * wet_frac[None])
    mixed = column_mix(forced, vert_kappa)
    coefficients = jnp.pad(jnp.stack([horiz_kappa, wet_frac]), ((0, 0), (1, 1), (1, 1)))
    tracers = mixed[:2]
    for pass_index in range(2):
        tracers = diffuse(jnp.pad(tracers, ((0, 0), (0, 0), (1, 1), (1, 1))), coefficients)
    ocean_next = jnp.concatenate([tracers, mixed[2:]], 0)
    surface = jnp.concatenate([ocean_next[:, 0] * wet_frac[None], wet_frac[None]], 0)
    surface_cells = surface.reshape(5, NXO, N_GY, TY).transpose(1, 2, 0, 3)
    picks = surface_cells[cell_x, cell_g].reshape(devices, NPAIR, 5, TY)

    def backward_one(inputs):
        device_picks, block_ids, tile_ids, device_weights = inputs
        chosen = device_weights[tile_ids].astype(jnp.float32)
        back = jnp.einsum('pab,pcb->pca', chosen, device_picks, precision=highest)
        sums = jax.ops.segment_sum(back, block_ids, num_segments=NBLK_DEV)
        values = sums[:, :4] / jnp.maximum(sums[:, 4:5], 0.1)
        return values.transpose(1, 0, 2).reshape(4, NBLK_DEV * ABLK)
    per_device = lax.map(backward_one, (picks, blocks_of, tiles_of, weights_all))
    atm_surface = per_device.transpose(1, 0, 2).reshape(4, ATM_COLS)
    return (ocean_next, atm_surface)
```

```python
import jax
import jax.numpy as jnp
from jax import lax
from jax.experimental import pallas as pl
from jax.experimental.pallas import tpu as pltpu
from jax.sharding import PartitionSpec as P

MESH = pl.DeviceIdType.MESH


def exchange_kernel(x_ref, o_ref, buf, out_sem, in_sem, own_sem, ready):
    gx, gy = lax.axis_index("gx"), lax.axis_index("gy")
    barrier = pltpu.get_barrier_semaphore()
    for r in range(1, 16):
        pl.semaphore_signal(barrier, inc=1, device_id=((gx + r) % 16, gy), device_id_type=MESH)
    for r in range(1, 8):
        pl.semaphore_signal(barrier, inc=1, device_id=(gx, (gy + r) % 8), device_id_type=MESH)
    pl.semaphore_wait(barrier, 22)
    for r in range(1, 8):
        pl.semaphore_signal(ready, inc=1, device_id=(gx, (gy + r) % 8), device_id_type=MESH)
    pl.semaphore_wait(ready, 7)

    def send(r, _):
        dx, dy = (gx + r // 8) % 16, (gy + r % 8) % 8
        pltpu.make_async_remote_copy(
            src_ref=x_ref.at[dx * 8 + dy],
            dst_ref=buf.at[r - 1],
            send_sem=out_sem,
            recv_sem=in_sem,
            device_id=(dx, dy),
            device_id_type=MESH,
        ).start()
        return 0

    lax.fori_loop(1, 128, send, 0)
    pltpu.make_async_copy(buf, buf, in_sem).wait()
    pltpu.make_async_copy(buf, buf, out_sem).wait()
    o_ref[gx * 8 + gy] = x_ref[gx * 8 + gy]

    def put(r, _):
        sx, sy = (gx + 16 - r // 8) % 16, (gy + 8 - r % 8) % 8
        o_ref[sx * 8 + sy] = buf[r - 1]
        return 0

    lax.fori_loop(1, 128, put, 0)


def exchange(x, number):
    shape = x.shape
    return pl.pallas_call(
        exchange_kernel,
        out_shape=jax.ShapeDtypeStruct(shape, x.dtype),
        in_specs=[pl.BlockSpec(memory_space=pltpu.VMEM)],
        out_specs=pl.BlockSpec(memory_space=pltpu.VMEM),
        scratch_shapes=[
            pltpu.VMEM((127,) + shape[1:], x.dtype),
            pltpu.SemaphoreType.DMA,
            pltpu.SemaphoreType.DMA,
            pltpu.SemaphoreType.DMA,
            pltpu.SemaphoreType.REGULAR,
        ],
        compiler_params=pltpu.CompilerParams(
            collective_id=number, has_side_effects=True, vmem_limit_bytes=16 << 20
        ),
        name="exchange",
    )(x)


def extended(shard, sides, width):
    for axis, dim in sides:
        count, length = (lax.axis_size(axis), shard.shape[dim])
        up = [(i, (i + 1) % count) for i in range(count - 1)]
        down = [(j, i) for i, j in up]
        last = lax.slice_in_dim(shard, length - width, length, axis=dim)
        leading = lax.slice_in_dim(shard, 0, width, axis=dim)
        before = lax.ppermute(last, axis, up)
        after = lax.ppermute(leading, axis, down)
        shard = jnp.concatenate([before, shard, after], axis=dim)
    return shard


def surface_flux(atm_state):
    wind_u = atm_state[0]
    wind_v = atm_state[1]
    speed = jnp.sqrt(wind_u * wind_u + wind_v * wind_v + 0.25)
    heat_flux = 0.5 * speed * (atm_state[2] - atm_state[5])
    water_flux = atm_state[4] - 0.3 * speed * atm_state[3]
    return jnp.stack([heat_flux, water_flux, 0.2 * speed * wind_u, 0.2 * speed * wind_v]).astype(
        jnp.bfloat16
    )


def column_mix(fields, vert_kappa):
    levels = vert_kappa.shape[0]
    face_coef = 0.5 * (vert_kappa[:-1] + vert_kappa[1:])
    zero_plane = jnp.zeros_like(vert_kappa[:1])
    above = jnp.concatenate([zero_plane, face_coef], 0)
    below = jnp.concatenate([face_coef, zero_plane], 0)
    diagonal = 1.0 + above + below
    upper_list = []
    rhs_list = []
    for level_index in range(levels):
        if level_index == 0:
            pivot_inv = 1.0 / diagonal[0]
            rhs_now = fields[:, 0] * pivot_inv
        else:
            pivot_inv = 1.0 / (diagonal[level_index] + above[level_index] * upper_list[-1])
            rhs_now = (fields[:, level_index] + above[level_index] * rhs_list[-1]) * pivot_inv
        upper_list.append(-below[level_index] * pivot_inv)
        rhs_list.append(rhs_now)
    solved = [rhs_list[-1]]
    for level_index in range(levels - 2, -1, -1):
        solved.append(rhs_list[level_index] - upper_list[level_index] * solved[-1])
    return jnp.stack(solved[::-1], 1)


def shifted(array, step_x, step_y):
    size_x = array.shape[-2]
    size_y = array.shape[-1]
    return array[..., 1 + step_x : size_x - 1 + step_x, 1 + step_y : size_y - 1 + step_y]


def diffuse(padded, coefficients):
    kappa_pad = coefficients[0]
    wet_pad = coefficients[1]
    centre = shifted(padded, 0, 0)
    kappa_mid = shifted(kappa_pad, 0, 0)
    wet_mid = shifted(wet_pad, 0, 0)
    result = centre
    for step_x, step_y in ((1, 0), (-1, 0), (0, 1), (0, -1)):
        face_coef = (
            0.25
            * (kappa_mid + shifted(kappa_pad, step_x, step_y))
            * wet_mid
            * shifted(wet_pad, step_x, step_y)
        )
        result = result + face_coef * (shifted(padded, step_x, step_y) - centre)
    return result


def local(
    atm_state,
    pair_block,
    pair_owner,
    pair_row,
    pair_tile,
    remap_weight,
    wet_mask,
    ocean_state,
    vert_kappa,
    horiz_kappa,
):
    highest = lax.Precision.HIGHEST
    grid_x = lax.axis_size("gx")
    grid_y = lax.axis_size("gy")
    devices = grid_x * grid_y
    npairs = pair_block.shape[0]
    capacity = max(2, 2 * npairs // devices)
    slot_count = devices * capacity
    tile_rows = ocean_state.shape[2]
    patch_width = ocean_state.shape[3]
    block_cols = remap_weight.shape[1]
    fluxes = surface_flux(atm_state)
    nblocks = fluxes.shape[1] // block_cols
    blocks = fluxes.reshape(4, nblocks, block_cols).transpose(1, 0, 2)
    tile_weights = remap_weight[pair_tile]
    contrib = jnp.einsum(
        "pca,pab->pcb", blocks[pair_block], tile_weights, preferred_element_type=jnp.float32
    )
    owner_ids = pair_owner[:, 0]
    owner_hits = (owner_ids[:, None] == jnp.arange(devices, dtype=jnp.int32)[None, :]).astype(
        jnp.int32
    )
    slot_rank = jnp.sum(owner_hits * (jnp.cumsum(owner_hits, 0) - 1), 1)
    send_slot = owner_ids * capacity + slot_rank
    outgoing = jnp.zeros((slot_count, 4, patch_width), jnp.float32).at[send_slot].set(contrib)
    out_rows = jnp.zeros((slot_count,), jnp.int32).at[send_slot].set(pair_row)
    arrived, in_rows = (
        exchange(outgoing.reshape(devices, capacity * 4, patch_width), 0),
        lax.all_to_all(out_rows, ("gx", "gy"), split_axis=0, concat_axis=0, tiled=True),
    )
    placing = (jnp.arange(tile_rows, dtype=jnp.int32)[:, None] == in_rows[None, :]).astype(
        jnp.float32
    )
    forcing = jnp.dot(
        placing,
        arrived.reshape(slot_count, 4 * patch_width),
        precision=highest,
        preferred_element_type=jnp.float32,
    )
    forcing = forcing.reshape(tile_rows, 4, patch_width).transpose(1, 0, 2)
    wet_frac = wet_mask.astype(jnp.float32)
    forced = ocean_state.at[:, 0].add(forcing * wet_frac[None])
    coef_pad = extended(jnp.stack([horiz_kappa, wet_frac]), (("gx", 1), ("gy", 2)), 2)
    coef_near = coef_pad[:, 1:-1, 1:-1]
    mixed = column_mix(forced, vert_kappa)
    tracers = mixed[:2]
    for pass_index in range(2):
        padded = extended(tracers, (("gx", 2), ("gy", 3)), 1)
        tracers = diffuse(padded, coef_near)
    ocean_next = jnp.concatenate([tracers, mixed[2:]], 0)
    surface = jnp.concatenate([ocean_next[:, 0] * wet_frac[None], wet_frac[None]], 0)
    sendback = surface.transpose(1, 0, 2)[in_rows]
    returned = exchange(sendback.reshape(devices, capacity * 5, patch_width), 1).reshape(slot_count, 5, patch_width)
    picks = returned[send_slot]
    picks_high = picks.astype(jnp.bfloat16)
    picks_low = (picks - picks_high.astype(jnp.float32)).astype(jnp.bfloat16)
    back = jnp.einsum("pab,pcb->pca", tile_weights, picks_high, preferred_element_type=jnp.float32)
    back = back + jnp.einsum(
        "pab,pcb->pca", tile_weights, picks_low, preferred_element_type=jnp.float32
    )
    member = (jnp.arange(nblocks, dtype=jnp.int32)[:, None] == pair_block[None, :]).astype(
        jnp.float32
    )
    sums = jnp.dot(
        member,
        back.reshape(npairs, 5 * block_cols),
        precision=highest,
        preferred_element_type=jnp.float32,
    )
    sums = sums.reshape(nblocks, 5, block_cols)
    values = sums[:, :4] / jnp.maximum(sums[:, 4:5], 0.1)
    atm_surface = values.transpose(1, 0, 2).reshape(4, nblocks * block_cols)
    return (ocean_next, atm_surface)


def solution(mesh):
    placed = (
        P(None, ("gx", "gy")),
        P(("gx", "gy")),
        P(("gx", "gy"), None),
        P(("gx", "gy")),
        P(("gx", "gy")),
        P(("gx", "gy"), None, None),
        P("gx", "gy"),
        P(None, None, "gx", "gy"),
        P(None, "gx", "gy"),
        P("gx", "gy"),
    )
    return jax.shard_map(
        local,
        mesh=mesh,
        in_specs=placed,
        out_specs=(P(None, None, "gx", "gy"), P(None, ("gx", "gy"))),
        check_vma=False,
    )
```

```python
import functools
import itertools
import random

import jax
import jax.numpy as jnp
from jax import lax
from jax.experimental import pallas as pl
from jax.experimental.pallas import tpu as pltpu
from jax.sharding import PartitionSpec as P

MESH = pl.DeviceIdType.MESH
F32 = jnp.float32
BF16 = jnp.bfloat16


def hops(step):
    return sum(min(v, 4 - v) for v in step[:3])


def send_order():
    steps = [s for s in itertools.product(range(4), range(4), range(4), range(2)) if any(s)]
    random.Random(0).shuffle(steps)
    return sorted(steps, key=lambda s: -hops(s))


ORDER = send_order()


def dot(a, b):
    return jnp.dot(a, b, preferred_element_type=F32)


def split(a):
    high = a.astype(BF16)
    return high, (a - high.astype(F32)).astype(BF16)


def iota(shape, dim):
    return lax.broadcasted_iota(jnp.int32, shape, dim)


def kernel(
    tile_s,
    block_s,
    owner_ref,
    row_ref,
    block_ref,
    atm_ref,
    wet_ref,
    kappa_ref,
    w_hbm,
    ocean_hbm,
    vert_hbm,
    ocean_out,
    atm_out,
    weights,
    planes,
    vert,
    gain,
    first,
    flux,
    masks,
    contrib,
    perm_t,
    row_out,
    row_in,
    send_f,
    recv_f,
    send_1,
    recv_1,
    send_2,
    recv_2,
    forcing,
    faces,
    edge_x,
    halo_x,
    edge_y,
    halo_y,
    coef_x,
    coef_hx,
    coef_y,
    coef_hy,
    picks,
    back,
    load_sem,
    out_sem,
    send_sem,
    recv_sem,
    halo_ss,
    halo_rs,
    ready,
):
    gx, gy = lax.axis_index("gx"), lax.axis_index("gy")
    me = gx * 8 + gy
    at_y = [((gx // 4 + d) % 4) * 4 for d in range(4)]
    at_x = [(gx % 4 + d) % 4 for d in range(4)]
    at_z = [((gy // 2 + d) % 4) * 2 for d in range(4)]
    at_c = [(gy % 2 + d) % 2 for d in range(2)]

    loads = [
        pltpu.make_async_copy(w_hbm, weights, load_sem.at[0]),
        pltpu.make_async_copy(vert_hbm, vert, load_sem.at[1]),
        pltpu.make_async_copy(ocean_hbm, planes, load_sem.at[2]),
    ]
    for copy in loads:
        copy.start()

    barrier = pltpu.get_barrier_semaphore()
    for r in range(1, 16):
        pl.semaphore_signal(barrier, inc=1, device_id=((gx + r) % 16, gy), device_id_type=MESH)
    for r in range(1, 8):
        pl.semaphore_signal(barrier, inc=1, device_id=(gx, (gy + r) % 8), device_id_type=MESH)

    def send_all(number, source, target, pitch, rows, steps, own):
        def block(ref, d):
            if pitch == 0:
                return ref.at[d]
            return ref.at[pl.ds(pl.multiple_of(d * pitch, 8), rows), :]

        if own:
            pltpu.make_async_copy(block(source, me), block(target, me), recv_sem.at[number]).start()
        for dy, dx, dz, dc in steps:
            tx, ty = at_y[dy] + at_x[dx], at_z[dz] + at_c[dc]
            pltpu.make_async_remote_copy(
                src_ref=block(source, tx * 8 + ty),
                dst_ref=block(target, me),
                send_sem=send_sem.at[number],
                recv_sem=recv_sem.at[number],
                device_id=(tx, ty),
                device_id_type=MESH,
            ).start()

    def wait_bytes(ref, sem):
        pltpu.make_async_copy(ref, ref, sem).wait()

    a = [atm_ref[i : i + 1, :] for i in range(6)]
    speed = jnp.sqrt(a[0] * a[0] + a[1] * a[1] + 0.25)
    rows4 = [
        0.5 * speed * (a[2] - a[5]),
        a[4] - 0.3 * speed * a[3],
        0.2 * speed * a[0],
        0.2 * speed * a[1],
    ]
    for b in range(48):
        flux[b] = jnp.concatenate(
            [jnp.broadcast_to(v[:, b * 128 : b * 128 + 128], (8, 128)) for v in rows4], axis=0
        ).astype(BF16)
    for i in range(8):
        masks[i] = jnp.where(iota((32, 128), 0) % 8 == i, 1.0, 0.0).astype(BF16)

    hit = (iota((128, 256), 0) == owner_ref[...]).astype(F32)
    before = (iota((256, 256), 0) < iota((256, 256), 1)).astype(BF16)
    rank = dot(hit.astype(BF16), before)
    perm = [jnp.where(rank == float(r), hit, 0.0) for r in range(4)]
    rows_f = row_ref[...].astype(F32) + 1.0
    lane128 = iota((128, 128), 1)
    row_msg = jnp.zeros((128, 128), F32)
    for r in range(4):
        at = jnp.sum(perm[r] * rows_f, axis=1, keepdims=True) - 1.0
        row_msg = jnp.where(lane128 == r, at, row_msg)
        perm_t[:, r * 128 : r * 128 + 128] = jnp.transpose(perm[r]).astype(BF16)
    row_out[...] = row_msg.reshape(128, 1, 128)

    wet = wet_ref[...].astype(F32)
    kappa = kappa_ref[...]
    row8 = iota((8, 128), 0)
    for side, r in ((0, 0), (1, 63)):
        coef_x[side] = jnp.where(row8 == 0, kappa[r : r + 1, :], wet[r : r + 1, :])
    lane = iota((64, 128), 1)
    low, high = lane == 0, lane == 127
    packed = jnp.where(low, pltpu.roll(kappa, 1, 1), pltpu.roll(wet, 2, 1))
    packed = jnp.where(lane == 2, pltpu.roll(kappa, 2, 1), packed)
    coef_y[...] = jnp.where(lane == 3, pltpu.roll(wet, 3, 1), packed)

    loads[0].wait()

    def forward(g, _):
        total = jnp.zeros((32, 128), F32)
        for i in range(8):
            p = g * 8 + i
            total = total + dot(flux[block_s[p]] * masks[i], weights[tile_s[p]])
        for c in range(4):
            contrib[pl.ds(pl.multiple_of(g * 8, 8), 8), c * 128 : c * 128 + 128] = total[
                c * 8 : c * 8 + 8
            ]
        return 0

    lax.fori_loop(0, 32, forward, 0)

    part_h, part_l = split(contrib[...])
    for r in range(4):
        pick = perm[r].astype(BF16)
        out = dot(pick, part_h) + dot(pick, part_l)
        for c in range(4):
            send_f[pl.ds(c * 4 + r, 128, stride=16), :] = out[:, c * 128 : c * 128 + 128]

    pl.semaphore_wait(barrier, 22)
    for r in range(1, 8):
        pl.semaphore_signal(ready, inc=1, device_id=(gx, (gy + r) % 8), device_id_type=MESH)

    near = [((gx + 15) % 16, gy), ((gx + 1) % 16, gy), (gx, (gy + 7) % 8), (gx, (gy + 1) % 8)]

    def swap(number, sources, targets):
        copies = []
        for side in range(4):
            copies.append(
                pltpu.make_async_remote_copy(
                    src_ref=sources[side],
                    dst_ref=targets[side ^ 1],
                    send_sem=halo_ss.at[number, side],
                    recv_sem=halo_rs.at[number, side ^ 1],
                    device_id=near[side],
                    device_id_type=MESH,
                )
            )
        for copy in copies:
            copy.start()
        return copies

    pl.semaphore_wait(ready, 7)
    send_all(0, send_f, recv_f, 16, 16, ORDER, True)
    coef_copies = swap(
        0,
        [coef_x.at[0], coef_x.at[1], coef_y, coef_y],
        [coef_hx.at[0], coef_hx.at[1], coef_hy.at[0], coef_hy.at[1]],
    )
    send_all(1, row_out, row_in, 0, 1, ORDER, True)

    loads[1].wait()
    loads[2].wait()

    def solve(i, _):
        def at(level):
            return pl.ds(pl.multiple_of(level * 64 + i * 8, 8), 8)

        kap = [vert[at(l), :] for l in range(16)]
        face = [0.5 * (kap[l] + kap[l + 1]) for l in range(15)]
        inv, upper = [], []
        for l in range(16):
            above = face[l - 1] if l > 0 else 0.0
            below = face[l] if l < 15 else 0.0
            diagonal = 1.0 + above + below
            inv.append(1.0 / (diagonal + above * upper[-1] if l > 0 else diagonal))
            upper.append(-below * inv[-1])
        for field in range(5):
            held = []
            for l in range(16):
                if field < 4:
                    value = planes[at(field * 16 + l), :]
                    value = value + face[l - 1] * held[-1] if l > 0 else value
                    held.append(value * inv[l])
                else:
                    held.append(face[l - 1] * held[-1] * inv[l] if l > 0 else inv[l])
            value = held[15]
            for l in range(15, -1, -1):
                value = held[l] - upper[l] * value if l < 15 else value
                if field < 4:
                    planes[at(field * 16 + l), :] = value
                else:
                    gain[at(l), :] = value
        return 0

    lax.fori_loop(0, 8, solve, 0)

    for copy in coef_copies:
        copy.wait()

    def edge_row(side, row, there):
        return jnp.where(there, coef_hx[side, row : row + 1, :], 0.0)

    row64 = iota((64, 128), 0)
    sides = []
    for side, shift, there, edge in (
        (0, 1, gx > 0, row64 == 0),
        (1, 63, gx < 15, row64 == 63),
    ):
        sides.append(
            [
                jnp.where(edge, edge_row(side, v, there), pltpu.roll(field, shift, 0))
                for v, field in enumerate((kappa, wet))
            ]
        )
    for side, shift, there, edge, lanes in (
        (0, 1, gy > 0, low, (0, 1)),
        (1, 127, gy < 7, high, (2, 3)),
    ):
        got = jnp.where(there, coef_hy[side], 0.0)
        goal = 0 if side == 0 else 127
        sides.append(
            [
                jnp.where(edge, pltpu.roll(got, (goal - lanes[v]) % 128, 1), pltpu.roll(field, shift, 1))
                for v, field in enumerate((kappa, wet))
            ]
        )
    for n, (kappa_n, wet_n) in enumerate(sides):
        faces[n] = 0.25 * (kappa + kappa_n) * wet * wet_n

    wait_bytes(row_in, recv_sem.at[1])
    rows_in = row_in[...].reshape(128, 128)
    rows_t = jnp.transpose(rows_in)
    x64 = iota((64, 128), 0).astype(F32)
    place = jnp.concatenate([(x64 == rows_t[r : r + 1, :]).astype(F32) for r in range(4)], axis=1)
    place = place.astype(BF16)
    twice = (lane128 % 64).astype(F32)
    fetch = [(rows_in[:, r : r + 1] == twice).astype(F32).astype(BF16) for r in range(4)]

    wait_bytes(recv_f, recv_sem.at[0])
    for c in range(4):
        got = jnp.concatenate(
            [recv_f[pl.ds(c * 4 + r, 128, stride=16), :] for r in range(4)], axis=0
        )
        got_h, got_l = split(got)
        forcing[c] = (dot(place, got_h) + dot(place, got_l)) * wet

    def mix_tracers(l, _):
        response = gain[pl.ds(pl.multiple_of(l * 64, 64), 64), :]
        for c in range(2):
            at = pl.ds(pl.multiple_of(c * 1024 + l * 64, 64), 64)
            planes[at, :] = planes[at, :] + response * forcing[c]
        return 0

    lax.fori_loop(0, 16, mix_tracers, 0)

    def send_edges(number, source):
        edge_x[number, 0] = source[pl.ds(0, 32, stride=64), :]
        edge_x[number, 1] = source[pl.ds(63, 32, stride=64), :]

        def pack(k, held):
            plane = source[pl.ds(pl.multiple_of(k * 64, 64), 64), :]
            held = jnp.where(lane == k, pltpu.roll(plane, k + 1, 1), held)
            return jnp.where(lane == k + 32, pltpu.roll(plane, k + 32, 1), held)

        edge_y[number] = lax.fori_loop(0, 32, pack, jnp.zeros((64, 128), F32))
        return swap(
            1 + number,
            [edge_x.at[number, 0], edge_x.at[number, 1], edge_y.at[number], edge_y.at[number]],
            [halo_x.at[number, 0], halo_x.at[number, 1], halo_y.at[number, 0], halo_y.at[number, 1]],
        )

    def diffuse(number, source, target, k):
        at = pl.ds(pl.multiple_of(k * 64, 64), 64)
        q = source[at, :]
        up = jnp.where(row64 == 0, halo_x[number, 0, pl.ds(k, 1), :], pltpu.roll(q, 1, 0))
        down = jnp.where(row64 == 63, halo_x[number, 1, pl.ds(k, 1), :], pltpu.roll(q, 63, 0))
        left = jnp.where(low, pltpu.roll(halo_y[number, 0], (128 - k) % 128, 1), pltpu.roll(q, 1, 1))
        right = jnp.where(high, pltpu.roll(halo_y[number, 1], 95 - k, 1), pltpu.roll(q, 127, 1))
        total = q
        for n, other in enumerate((up, down, left, right)):
            total = total + faces[n] * (other - q)
        target[at, :] = total

    def give_back(source, target, pitch):
        parts = [split(v) for v in source]
        stacked = jnp.concatenate(
            [jnp.concatenate([h, l], axis=0) for h, l in parts], axis=1
        )
        for r in range(4):
            out = dot(fetch[r], stacked)
            for c in range(len(source)):
                target[pl.ds(c * 4 + r, 128, stride=pitch), :] = out[:, c * 128 : c * 128 + 128]

    copies_1 = send_edges(0, planes)
    response = gain[0:64, :]
    give_back(
        [(planes[c * 1024 : c * 1024 + 64, :] + response * forcing[c]) * wet for c in (2, 3)] + [wet],
        send_1,
        16,
    )
    send_all(2, send_1, recv_1, 16, 12, ORDER[:64], True)
    for copy in copies_1:
        copy.wait()

    def pass_1(k, _):
        diffuse(0, planes, first, k)
        return 0

    lax.fori_loop(0, 32, pass_1, 0)
    copies_2 = send_edges(1, first)
    send_all(2, send_1, recv_1, 16, 12, ORDER[64:], False)
    for copy in copies_2:
        copy.wait()
    diffuse(1, first, planes, 0)
    diffuse(1, first, planes, 16)
    give_back([planes[c * 1024 : c * 1024 + 64, :] * wet for c in (0, 1)], send_2, 8)
    send_all(3, send_2, recv_2, 8, 8, ORDER, True)

    def pass_2(l, _):
        diffuse(1, first, planes, l)
        diffuse(1, first, planes, l + 16)
        return 0

    lax.fori_loop(1, 16, pass_2, 0)

    def mix_flow(l, _):
        response = gain[pl.ds(pl.multiple_of(l * 64, 64), 64), :]
        for c in (2, 3):
            at = pl.ds(pl.multiple_of(c * 1024 + l * 64, 64), 64)
            planes[at, :] = planes[at, :] + response * forcing[c]
        return 0

    lax.fori_loop(0, 16, mix_flow, 0)
    store = pltpu.make_async_copy(planes, ocean_out, out_sem)
    store.start()

    wait_bytes(recv_1.at[pl.ds(0, 1536), :], recv_sem.at[2])

    def take(source, pitch, c, plane):
        got = jnp.concatenate(
            [source[pl.ds(c * 4 + r, 128, stride=pitch), :] for r in range(4)], axis=0
        )
        for half, part in enumerate(split(got)):
            picks[half * 5 + plane] = dot(perm_t[...], part)

    for c, plane in ((0, 2), (1, 3), (2, 4)):
        take(recv_1, 16, c, plane)
    wait_bytes(recv_2, recv_sem.at[3])
    for c in range(2):
        take(recv_2, 8, c, c)

    row80 = iota((80, 128), 0) % 8

    def backward(g, _):
        at = pl.ds(pl.multiple_of(g * 8, 8), 8)
        rows = jnp.concatenate([picks[n, at, :] for n in range(10)], axis=0)
        total = jnp.zeros((80, 128), F32)
        for i in range(8):
            mine = jnp.where(row80 == i, rows, 0.0).astype(BF16)
            total = total + lax.dot_general(
                mine,
                weights[tile_s[g * 8 + i]],
                (((1,), (1,)), ((), ())),
                preferred_element_type=F32,
            )
        for c in range(5):
            back[c, at, :] = total[c * 8 : c * 8 + 8] + total[40 + c * 8 : 48 + c * 8]
        return 0

    lax.fori_loop(0, 32, backward, 0)

    of_block = iota((192, 256), 0) // 4 == block_ref[...]
    plane_of = iota((192, 256), 0) % 4
    num = jnp.zeros((192, 128), F32)
    for c in range(4):
        member = jnp.where(of_block & (plane_of == c), 1.0, 0.0).astype(BF16)
        for part in split(back[c]):
            num = num + dot(member, part)
    den = jnp.zeros((192, 128), F32)
    member = jnp.where(of_block, 1.0, 0.0).astype(BF16)
    for part in split(back[4]):
        den = den + dot(member, part)
    atm_out[...] = num / jnp.maximum(den, 0.1)

    wait_bytes(send_f.at[pl.ds(0, 127 * 16), :], send_sem.at[0])
    wait_bytes(row_out.at[pl.ds(0, 127)], send_sem.at[1])
    wait_bytes(send_1.at[pl.ds(0, 127 * 12), :], send_sem.at[2])
    wait_bytes(send_2.at[pl.ds(0, 127 * 8), :], send_sem.at[3])
    store.wait()


def local(
    atm_state,
    pair_block,
    pair_owner,
    pair_row,
    pair_tile,
    remap_weight,
    wet_mask,
    ocean_state,
    vert_kappa,
    horiz_kappa,
):
    vmem = pl.BlockSpec(memory_space=pltpu.VMEM)
    smem = pl.BlockSpec(memory_space=pltpu.SMEM)
    hbm = pl.BlockSpec(memory_space=pl.ANY)
    dma = pltpu.SemaphoreType.DMA

    def buffer(*shape, dtype=F32):
        return pltpu.VMEM(shape, dtype)

    ocean, atm = pl.pallas_call(
        kernel,
        out_shape=(
            jax.ShapeDtypeStruct((4096, 128), F32),
            jax.ShapeDtypeStruct((192, 128), F32),
        ),
        in_specs=[smem, smem, vmem, vmem, vmem, vmem, vmem, vmem, hbm, hbm, hbm],
        out_specs=(hbm, vmem),
        scratch_shapes=[
            buffer(128, 128, 128, dtype=BF16),
            buffer(4096, 128),
            buffer(1024, 128),
            buffer(1024, 128),
            buffer(2048, 128),
            buffer(48, 32, 128, dtype=BF16),
            buffer(8, 32, 128, dtype=BF16),
            buffer(256, 512),
            buffer(256, 512, dtype=BF16),
            buffer(128, 1, 128),
            buffer(128, 1, 128),
            buffer(2048, 128),
            buffer(2048, 128),
            buffer(2048, 128),
            buffer(2048, 128),
            buffer(1024, 128),
            buffer(1024, 128),
            buffer(4, 64, 128),
            buffer(4, 64, 128),
            buffer(2, 2, 32, 128),
            buffer(2, 2, 32, 128),
            buffer(2, 64, 128),
            buffer(2, 2, 64, 128),
            buffer(2, 8, 128),
            buffer(2, 8, 128),
            buffer(64, 128),
            buffer(2, 64, 128),
            buffer(10, 256, 128),
            buffer(5, 256, 128),
            dma((3,)),
            dma,
            dma((4,)),
            dma((4,)),
            dma((3, 4)),
            dma((3, 4)),
            pltpu.SemaphoreType.REGULAR,
        ],
        compiler_params=pltpu.CompilerParams(
            collective_id=0, has_side_effects=True, vmem_limit_bytes=40 << 20
        ),
        name="couple",
    )(
        pair_tile,
        pair_block,
        pair_owner.reshape(1, 256),
        pair_row.reshape(1, 256),
        pair_block.reshape(1, 256),
        atm_state,
        wet_mask,
        horiz_kappa,
        remap_weight,
        ocean_state.reshape(4096, 128),
        vert_kappa.reshape(1024, 128),
    )
    ocean_next = ocean.reshape(4, 16, 64, 128)
    atm_surface = atm.reshape(48, 4, 128).transpose(1, 0, 2).reshape(4, 6144)
    return (ocean_next, atm_surface)


def solution(mesh):
    placed = (
        P(None, ("gx", "gy")),
        P(("gx", "gy")),
        P(("gx", "gy"), None),
        P(("gx", "gy")),
        P(("gx", "gy")),
        P(("gx", "gy"), None, None),
        P("gx", "gy"),
        P(None, None, "gx", "gy"),
        P(None, "gx", "gy"),
        P("gx", "gy"),
    )
    return jax.shard_map(
        local,
        mesh=mesh,
        in_specs=placed,
        out_specs=(P(None, None, "gx", "gy"), P(None, ("gx", "gy"))),
        check_vma=False,
    )
```

```python
import itertools
import random

import jax
import jax.numpy as jnp
from jax import lax
from jax.experimental import pallas as pl
from jax.experimental.pallas import tpu as pltpu
from jax.sharding import PartitionSpec as P

MESH = pl.DeviceIdType.MESH
F32 = jnp.float32
BF16 = jnp.bfloat16


def hops(step):
    return sum(min(v, 4 - v) for v in step[:3])


def send_order():
    steps = [s for s in itertools.product(range(4), range(4), range(4), range(2)) if any(s)]
    random.Random(0).shuffle(steps)
    return sorted(steps, key=lambda s: -hops(s))


ORDER = send_order()


def dot(a, b):
    return jnp.dot(a, b, preferred_element_type=F32)


def split(a):
    high = a.astype(BF16)
    return high, (a - high.astype(F32)).astype(BF16)


def iota(shape, dim):
    return lax.broadcasted_iota(jnp.int32, shape, dim)


def kernel(
    tile_hbm,
    block_hbm,
    owner_hbm,
    row_hbm,
    atm_hbm,
    wet_hbm,
    kappa_hbm,
    w_hbm,
    ocean_hbm,
    vert_hbm,
    ocean_out,
    atm_out,
    tile_s,
    block_s,
    owner_ref,
    row_ref,
    block_ref,
    atm_ref,
    wet_ref,
    kappa_ref,
    atm_held,
    weights,
    planes,
    vert,
    gain,
    first,
    flux,
    contrib,
    perm_t,
    row_held,
    row_out,
    row_mid,
    row_next,
    row_in,
    send_f,
    recv_f,
    send_w,
    recv_w,
    send_1,
    recv_1,
    send_2,
    recv_2,
    forcing,
    faces,
    edge_x,
    halo_x,
    edge_y,
    halo_y,
    sides_y,
    coef_x,
    coef_hx,
    coef_y,
    coef_hy,
    picks,
    back,
    load_sem,
    out_sem,
    send_sem,
    recv_sem,
    halo_ss,
    halo_rs,
    row_ss,
    row_rs,
    ready,
):
    gx, gy = lax.axis_index("gx"), lax.axis_index("gy")
    me = gx * 8 + gy
    at_y = [((gx // 4 + d) % 4) * 4 for d in range(4)]
    at_x = [(gx % 4 + d) % 4 for d in range(4)]
    at_z = [((gy // 2 + d) % 4) * 2 for d in range(4)]
    at_c = [(gy % 2 + d) % 2 for d in range(2)]

    loads = [
        pltpu.make_async_copy(source, target, load_sem.at[i])
        for i, (source, target) in enumerate(
            (
                (owner_hbm, owner_ref),
                (row_hbm, row_ref),
                (atm_hbm, atm_ref),
                (w_hbm, weights),
                (tile_hbm, tile_s),
                (block_hbm, block_s),
                (block_hbm, block_ref),
                (wet_hbm, wet_ref),
                (kappa_hbm, kappa_ref),
                (vert_hbm, vert),
                (ocean_hbm, planes),
            )
        )
    ]
    for copy in loads:
        copy.start()

    barrier = pltpu.get_barrier_semaphore()
    for r in range(1, 16):
        pl.semaphore_signal(barrier, inc=1, device_id=((gx + r) % 16, gy), device_id_type=MESH)
    for r in range(1, 8):
        pl.semaphore_signal(barrier, inc=1, device_id=(gx, (gy + r) % 8), device_id_type=MESH)

    def send_all(number, source, target, pitch, rows, steps, own):
        def block(ref, d):
            return ref.at[pl.ds(pl.multiple_of(d * pitch, 8), rows), :]

        if own:
            pltpu.make_async_copy(block(source, me), block(target, me), recv_sem.at[number]).start()
        for dy, dx, dz, dc in steps:
            tx, ty = at_y[dy] + at_x[dx], at_z[dz] + at_c[dc]
            pltpu.make_async_remote_copy(
                src_ref=block(source, tx * 8 + ty),
                dst_ref=block(target, me),
                send_sem=send_sem.at[number],
                recv_sem=recv_sem.at[number],
                device_id=(tx, ty),
                device_id_type=MESH,
            ).start()

    def wait_bytes(ref, sem):
        pltpu.make_async_copy(ref, ref, sem).wait()

    loads[2].wait()
    a = [atm_ref[i : i + 1, :] for i in range(6)]
    speed = jnp.sqrt(a[0] * a[0] + a[1] * a[1] + 0.25)
    rows4 = [
        0.5 * speed * (a[2] - a[5]),
        a[4] - 0.3 * speed * a[3],
        0.2 * speed * a[0],
        0.2 * speed * a[1],
    ]
    blank = jnp.zeros((12, 128), F32)
    for b in range(48):
        flux[b] = jnp.concatenate(
            [v[:, b * 128 : b * 128 + 128] for v in rows4] + [blank], axis=0
        ).astype(BF16)

    loads[0].wait()
    loads[1].wait()
    hit = (iota((128, 256), 0) == owner_ref[...]).astype(F32)
    before = (iota((256, 256), 0) < iota((256, 256), 1)).astype(BF16)
    rank = dot(hit.astype(BF16), before)
    perm = [jnp.where(rank == float(r), hit, 0.0) for r in range(4)]
    rows_f = row_ref[...].astype(F32) + 1.0
    lane128 = iota((128, 128), 1)
    row_msg = jnp.zeros((128, 128), F32)
    for r in range(4):
        at = jnp.sum(perm[r] * rows_f, axis=1, keepdims=True) - 1.0
        row_msg = jnp.where(lane128 == r, at, row_msg)
        perm_t[:, r * 128 : r * 128 + 128] = jnp.transpose(perm[r]).astype(BF16)
    row_held[...] = row_msg
    for t in range(8):
        row_out[t] = row_held[pl.ds(t, 16, stride=8), :]

    loads[7].wait()
    loads[8].wait()
    wet = wet_ref[...].astype(F32)
    kappa = kappa_ref[...]
    row8 = iota((8, 128), 0)
    for side, r in ((0, 0), (1, 63)):
        coef_x[side] = jnp.where(row8 == 0, kappa[r : r + 1, :], wet[r : r + 1, :])
    lane = iota((64, 128), 1)
    low, high = lane == 0, lane == 127
    packed = jnp.where(low, pltpu.roll(kappa, 1, 1), pltpu.roll(wet, 2, 1))
    packed = jnp.where(lane == 2, pltpu.roll(kappa, 2, 1), packed)
    coef_y[...] = jnp.where(lane == 3, pltpu.roll(wet, 3, 1), packed)

    for i in (3, 4, 5):
        loads[i].wait()

    def forward(g, _):
        for i in range(16):
            p = g * 16 + i
            out = dot(flux[block_s[0, p]], weights[tile_s[0, p]])
            contrib[pl.ds(pl.multiple_of(p * 8, 8), 8), :] = out[0:8]
        return 0

    lax.fori_loop(0, 6, forward, 0)

    pl.semaphore_wait(barrier, 22)
    for r in range(1, 8):
        pl.semaphore_signal(ready, inc=1, device_id=(gx, (gy + r) % 8), device_id_type=MESH)
    pltpu.make_async_copy(row_out.at[gy], row_mid.at[gy], row_rs.at[0]).start()
    for r in range(1, 8):
        t = (gy + r) % 8
        pltpu.make_async_remote_copy(
            src_ref=row_out.at[t],
            dst_ref=row_mid.at[gy],
            send_sem=row_ss.at[0],
            recv_sem=row_rs.at[0],
            device_id=(gx, t),
            device_id_type=MESH,
        ).start()

    lax.fori_loop(6, 16, forward, 0)

    wait_bytes(row_mid, row_rs.at[0])
    mid = row_mid[...].reshape(128, 128)
    row_held[...] = mid
    for t in range(16):
        row_next[t] = row_held[pl.ds(t, 8, stride=16), :]
    pltpu.make_async_copy(row_next.at[gx], row_in.at[gx], row_rs.at[1]).start()
    for r in range(1, 16):
        t = (gx + r) % 16
        pltpu.make_async_remote_copy(
            src_ref=row_next.at[t],
            dst_ref=row_in.at[gx],
            send_sem=row_ss.at[1],
            recv_sem=row_rs.at[1],
            device_id=(t, gy),
            device_id_type=MESH,
        ).start()

    part_h, part_l = split(
        jnp.concatenate([contrib[pl.ds(c, 256, stride=8), :] for c in range(4)], axis=1)
    )
    for r in range(4):
        pick = perm[r].astype(BF16)
        out = dot(pick, part_h) + dot(pick, part_l)
        for c in range(4):
            send_f[pl.ds(c * 4 + r, 128, stride=16), :] = out[:, c * 128 : c * 128 + 128]

    near = [((gx + 15) % 16, gy), ((gx + 1) % 16, gy), (gx, (gy + 7) % 8), (gx, (gy + 1) % 8)]

    def swap(number, sources, targets):
        copies = []
        for side in range(4):
            copies.append(
                pltpu.make_async_remote_copy(
                    src_ref=sources[side],
                    dst_ref=targets[side ^ 1],
                    send_sem=halo_ss.at[number, side],
                    recv_sem=halo_rs.at[number, side ^ 1],
                    device_id=near[side],
                    device_id_type=MESH,
                )
            )
        for copy in copies:
            copy.start()
        return copies

    pl.semaphore_wait(ready, 7)
    send_all(0, send_f, recv_f, 16, 16, ORDER, True)
    coef_copies = swap(
        0,
        [coef_x.at[0], coef_x.at[1], coef_y, coef_y],
        [coef_hx.at[0], coef_hx.at[1], coef_hy.at[0], coef_hy.at[1]],
    )

    wait_bytes(row_in, row_rs.at[1])
    rows_in = row_in[...].reshape(128, 128)
    rows_t = jnp.transpose(rows_in)
    x64 = iota((64, 128), 0).astype(F32)
    place = jnp.concatenate([(x64 == rows_t[r : r + 1, :]).astype(F32) for r in range(4)], axis=1)
    place = place.astype(BF16)
    twice = (lane128 % 64).astype(F32)
    fetch = [(rows_in[:, r : r + 1] == twice).astype(F32).astype(BF16) for r in range(4)]

    def give_back(source, target, pitch):
        parts = [split(v) for v in source]
        stacked = jnp.concatenate([jnp.concatenate([h, l], axis=0) for h, l in parts], axis=1)
        for r in range(4):
            out = dot(fetch[r], stacked)
            for c in range(len(source)):
                target[pl.ds(c * 4 + r, 128, stride=pitch), :] = out[:, c * 128 : c * 128 + 128]

    give_back([wet], send_w, 8)
    send_all(1, send_w, recv_w, 8, 4, ORDER, True)

    loads[9].wait()
    loads[10].wait()

    def solve(i, _):
        def at(level):
            return pl.ds(pl.multiple_of(level * 64 + i * 8, 8), 8)

        kap = [vert[at(l), :] for l in range(16)]
        face = [0.5 * (kap[l] + kap[l + 1]) for l in range(15)]
        inv, upper = [], []
        for l in range(16):
            above = face[l - 1] if l > 0 else 0.0
            below = face[l] if l < 15 else 0.0
            diagonal = 1.0 + above + below
            inv.append(1.0 / (diagonal + above * upper[-1] if l > 0 else diagonal))
            upper.append(-below * inv[-1])
        for field in range(5):
            held = []
            for l in range(16):
                if field < 4:
                    value = planes[at(field * 16 + l), :]
                    value = value + face[l - 1] * held[-1] if l > 0 else value
                    held.append(value * inv[l])
                else:
                    held.append(face[l - 1] * held[-1] * inv[l] if l > 0 else inv[l])
            value = held[15]
            for l in range(15, -1, -1):
                value = held[l] - upper[l] * value if l < 15 else value
                if field < 4:
                    planes[at(field * 16 + l), :] = value
                else:
                    gain[at(l), :] = value
        return 0

    lax.fori_loop(0, 8, solve, 0)

    for copy in coef_copies:
        copy.wait()

    def edge_row(side, row, there):
        return jnp.where(there, coef_hx[side, row : row + 1, :], 0.0)

    row64 = iota((64, 128), 0)
    sides = []
    for side, shift, there, edge in (
        (0, 1, gx > 0, row64 == 0),
        (1, 63, gx < 15, row64 == 63),
    ):
        sides.append(
            [
                jnp.where(edge, edge_row(side, v, there), pltpu.roll(field, shift, 0))
                for v, field in enumerate((kappa, wet))
            ]
        )
    for side, shift, there, edge, lanes in (
        (0, 1, gy > 0, low, (0, 1)),
        (1, 127, gy < 7, high, (2, 3)),
    ):
        got = jnp.where(there, coef_hy[side], 0.0)
        goal = 0 if side == 0 else 127
        sides.append(
            [
                jnp.where(edge, pltpu.roll(got, (goal - lanes[v]) % 128, 1), pltpu.roll(field, shift, 1))
                for v, field in enumerate((kappa, wet))
            ]
        )
    for n, (kappa_n, wet_n) in enumerate(sides):
        faces[n] = 0.25 * (kappa + kappa_n) * wet * wet_n

    wait_bytes(recv_f, recv_sem.at[0])
    for c in range(4):
        got = jnp.concatenate(
            [recv_f[pl.ds(c * 4 + r, 128, stride=16), :] for r in range(4)], axis=0
        )
        got_h, got_l = split(got)
        forcing[c] = (dot(place, got_h) + dot(place, got_l)) * wet

    def mix_tracers(l, _):
        response = gain[pl.ds(pl.multiple_of(l * 64, 64), 64), :]
        for c in range(2):
            at = pl.ds(pl.multiple_of(c * 1024 + l * 64, 64), 64)
            planes[at, :] = planes[at, :] + response * forcing[c]
        return 0

    lax.fori_loop(0, 16, mix_tracers, 0)

    pair = lane // 2

    def send_edges(number, source):
        edge_x[number, 0] = source[pl.ds(0, 32, stride=64), :]
        edge_x[number, 1] = source[pl.ds(63, 32, stride=64), :]

        def pack(k, held):
            plane = source[pl.ds(pl.multiple_of(k * 64, 64), 64), :]
            return jnp.where(pair == k, pltpu.roll(plane, 2 * k + 1, 1), held)

        edge_y[number] = lax.fori_loop(0, 32, pack, jnp.zeros((64, 128), F32), unroll=8)
        return swap(
            1 + number,
            [edge_x.at[number, 0], edge_x.at[number, 1], edge_y.at[number], edge_y.at[number]],
            [halo_x.at[number, 0], halo_x.at[number, 1], halo_y.at[number, 0], halo_y.at[number, 1]],
        )

    def join_sides(number):
        left, right = halo_y[number, 0], halo_y[number, 1]
        sides_y[number] = jnp.where(lane % 2 == 1, pltpu.roll(left, 1, 1), pltpu.roll(right, 127, 1))

    def diffuse(number, source, target, k):
        at = pl.ds(pl.multiple_of(k * 64, 64), 64)
        q = source[at, :]
        up = jnp.where(row64 == 0, halo_x[number, 0, pl.ds(k, 1), :], pltpu.roll(q, 1, 0))
        down = jnp.where(row64 == 63, halo_x[number, 1, pl.ds(k, 1), :], pltpu.roll(q, 63, 0))
        beside = pltpu.roll(sides_y[number], 127 - 2 * k, 1)
        left = jnp.where(low, beside, pltpu.roll(q, 1, 1))
        right = jnp.where(high, beside, pltpu.roll(q, 127, 1))
        total = q
        for n, other in enumerate((up, down, left, right)):
            total = total + faces[n] * (other - q)
        target[at, :] = total

    copies_1 = send_edges(0, planes)
    response = gain[0:64, :]
    give_back(
        [(planes[c * 1024 : c * 1024 + 64, :] + response * forcing[c]) * wet for c in (2, 3)],
        send_1,
        8,
    )
    send_all(2, send_1, recv_1, 8, 8, ORDER[:64], True)
    for copy in copies_1:
        copy.wait()
    join_sides(0)

    def pass_1(k, _):
        diffuse(0, planes, first, k)
        return 0

    lax.fori_loop(0, 32, pass_1, 0, unroll=4)
    copies_2 = send_edges(1, first)
    send_all(2, send_1, recv_1, 8, 8, ORDER[64:], False)
    for copy in copies_2:
        copy.wait()
    join_sides(1)
    diffuse(1, first, planes, 0)
    diffuse(1, first, planes, 16)
    give_back([planes[c * 1024 : c * 1024 + 64, :] * wet for c in (0, 1)], send_2, 8)
    send_all(3, send_2, recv_2, 8, 8, ORDER, True)

    def pass_2(l, _):
        diffuse(1, first, planes, l)
        diffuse(1, first, planes, l + 16)
        return 0

    lax.fori_loop(1, 16, pass_2, 0, unroll=3)

    def mix_flow(l, _):
        response = gain[pl.ds(pl.multiple_of(l * 64, 64), 64), :]
        for c in (2, 3):
            at = pl.ds(pl.multiple_of(c * 1024 + l * 64, 64), 64)
            planes[at, :] = planes[at, :] + response * forcing[c]
        return 0

    lax.fori_loop(0, 16, mix_flow, 0)
    store = pltpu.make_async_copy(planes, ocean_out, out_sem.at[0])
    store.start()


    def take(source, pitch, c, plane):
        got = jnp.concatenate(
            [source[pl.ds(c * 4 + r, 128, stride=pitch), :] for r in range(4)], axis=0
        )
        for half, part in enumerate(split(got)):
            picks[pl.ds(half * 8 + plane, 256, stride=16), :] = dot(perm_t[...], part)

    wait_bytes(recv_w.at[pl.ds(0, 512), :], recv_sem.at[1])
    take(recv_w, 8, 0, 4)
    wait_bytes(recv_1, recv_sem.at[2])
    for c in range(2):
        take(recv_1, 8, c, c + 2)
    wait_bytes(recv_2, recv_sem.at[3])
    for c in range(2):
        take(recv_2, 8, c, c)

    def backward(g, _):
        for i in range(16):
            p = g * 16 + i
            out = lax.dot_general(
                picks[pl.ds(pl.multiple_of(p * 16, 16), 16), :].astype(BF16),
                weights[tile_s[0, p]],
                (((1,), (1,)), ((), ())),
                preferred_element_type=F32,
            )
            back[pl.ds(pl.multiple_of(p * 8, 8), 8), :] = out[0:8] + out[8:16]
        return 0

    lax.fori_loop(0, 16, backward, 0)

    loads[6].wait()
    of_block = iota((192, 256), 0) // 4 == block_ref[...]
    plane_of = iota((192, 256), 0) % 4
    num = jnp.zeros((192, 128), F32)
    for c in range(4):
        member = jnp.where(of_block & (plane_of == c), 1.0, 0.0).astype(BF16)
        for part in split(back[pl.ds(c, 256, stride=8), :]):
            num = num + dot(member, part)
    den = jnp.zeros((192, 128), F32)
    member = jnp.where(of_block, 1.0, 0.0).astype(BF16)
    for part in split(back[pl.ds(4, 256, stride=8), :]):
        den = den + dot(member, part)
    atm_held[...] = num / jnp.maximum(den, 0.1)
    store_atm = pltpu.make_async_copy(atm_held, atm_out, out_sem.at[1])
    store_atm.start()

    wait_bytes(send_f.at[pl.ds(0, 127 * 16), :], send_sem.at[0])
    wait_bytes(row_out.at[pl.ds(0, 7)], row_ss.at[0])
    wait_bytes(row_next.at[pl.ds(0, 15)], row_ss.at[1])
    wait_bytes(send_w.at[pl.ds(0, 127 * 4), :], send_sem.at[1])
    wait_bytes(send_1.at[pl.ds(0, 127 * 8), :], send_sem.at[2])
    wait_bytes(send_2.at[pl.ds(0, 127 * 8), :], send_sem.at[3])
    store.wait()
    store_atm.wait()


def hand_over(ocean_in, atm_in, ocean_out, atm_out, held, in_sem, out_sem):
    parts = [pl.ds(i * 512, 512) for i in range(8)]
    loads = [
        pltpu.make_async_copy(ocean_in.at[at, :], held.at[at, :], in_sem.at[i])
        for i, at in enumerate(parts)
    ]
    stores = [
        pltpu.make_async_copy(held.at[at, :], ocean_out.at[at, :], out_sem.at[i])
        for i, at in enumerate(parts)
    ]
    for copy in loads:
        copy.start()
    for b in range(48):
        atm_out[:, b * 128 : b * 128 + 128] = atm_in[b * 4 : b * 4 + 4, :]
    for load, store in zip(loads, stores):
        load.wait()
        store.start()
    for copy in stores:
        copy.wait()


def local(
    atm_state,
    pair_block,
    pair_owner,
    pair_row,
    pair_tile,
    remap_weight,
    wet_mask,
    ocean_state,
    vert_kappa,
    horiz_kappa,
):
    hbm = pl.BlockSpec(memory_space=pl.ANY)
    dma = pltpu.SemaphoreType.DMA

    def buffer(*shape, dtype=F32):
        return pltpu.VMEM(shape, dtype)

    ocean, atm = pl.pallas_call(
        kernel,
        out_shape=(
            jax.ShapeDtypeStruct((4096, 128), F32),
            jax.ShapeDtypeStruct((192, 128), F32),
        ),
        in_specs=[hbm] * 10,
        out_specs=(hbm, hbm),
        scratch_shapes=[
            pltpu.SMEM((1, 256), jnp.int32),
            pltpu.SMEM((1, 256), jnp.int32),
            buffer(1, 256, dtype=jnp.int32),
            buffer(1, 256, dtype=jnp.int32),
            buffer(1, 256, dtype=jnp.int32),
            buffer(6, 6144),
            buffer(64, 128, dtype=jnp.int32),
            buffer(64, 128),
            buffer(192, 128),
            buffer(128, 128, 128, dtype=BF16),
            buffer(4096, 128),
            buffer(1024, 128),
            buffer(1024, 128),
            buffer(2048, 128),
            buffer(48, 16, 128, dtype=BF16),
            buffer(2048, 128),
            buffer(256, 512, dtype=BF16),
            buffer(128, 128),
            buffer(8, 16, 128),
            buffer(8, 16, 128),
            buffer(16, 8, 128),
            buffer(16, 8, 128),
            buffer(2048, 128),
            buffer(2048, 128),
            buffer(1024, 128),
            buffer(1024, 128),
            buffer(1024, 128),
            buffer(1024, 128),
            buffer(1024, 128),
            buffer(1024, 128),
            buffer(4, 64, 128),
            buffer(4, 64, 128),
            buffer(2, 2, 32, 128),
            buffer(2, 2, 32, 128),
            buffer(2, 64, 128),
            buffer(2, 2, 64, 128),
            buffer(2, 64, 128),
            buffer(2, 8, 128),
            buffer(2, 8, 128),
            buffer(64, 128),
            buffer(2, 64, 128),
            buffer(4096, 128),
            buffer(2048, 128),
            dma((11,)),
            dma((2,)),
            dma((4,)),
            dma((4,)),
            dma((3, 4)),
            dma((3, 4)),
            dma((2,)),
            dma((2,)),
            pltpu.SemaphoreType.REGULAR,
        ],
        compiler_params=pltpu.CompilerParams(
            collective_id=0, has_side_effects=True, vmem_limit_bytes=63 << 20
        ),
        name="couple",
    )(
        pair_tile.reshape(1, 256),
        pair_block.reshape(1, 256),
        pair_owner.reshape(1, 256),
        pair_row.reshape(1, 256),
        atm_state,
        wet_mask,
        horiz_kappa,
        remap_weight,
        ocean_state.reshape(4096, 128),
        vert_kappa.reshape(1024, 128),
    )
    vmem = pl.BlockSpec(memory_space=pltpu.VMEM)
    ocean_next, atm_surface = pl.pallas_call(
        hand_over,
        out_shape=(
            jax.ShapeDtypeStruct((4096, 128), F32),
            jax.ShapeDtypeStruct((4, 6144), F32),
        ),
        in_specs=[hbm, vmem],
        out_specs=(hbm, vmem),
        scratch_shapes=[buffer(4096, 128), dma((8,)), dma((8,))],
        name="hand_over",
    )(ocean, atm)
    return (ocean_next.reshape(4, 16, 64, 128), atm_surface)


def solution(mesh):
    placed = (
        P(None, ("gx", "gy")),
        P(("gx", "gy")),
        P(("gx", "gy"), None),
        P(("gx", "gy")),
        P(("gx", "gy")),
        P(("gx", "gy"), None, None),
        P("gx", "gy"),
        P(None, None, "gx", "gy"),
        P(None, "gx", "gy"),
        P("gx", "gy"),
    )
    return jax.shard_map(
        local,
        mesh=mesh,
        in_specs=placed,
        out_specs=(P(None, None, "gx", "gy"), P(None, ("gx", "gy"))),
        check_vma=False,
    )
```

```python
import itertools
import random

import jax
import jax.numpy as jnp
from jax import lax
from jax.experimental import pallas as pl
from jax.experimental.pallas import tpu as pltpu
from jax.sharding import PartitionSpec as P

MESH = pl.DeviceIdType.MESH
F32 = jnp.float32
BF16 = jnp.bfloat16


def hops(step):
    return sum(min(v, 4 - v) for v in step[:3])


def send_order():
    steps = [s for s in itertools.product(range(4), range(4), range(4), range(2)) if any(s)]
    random.Random(0).shuffle(steps)
    return sorted(steps, key=lambda s: -hops(s))


ORDER = send_order()


def dot(a, b):
    return jnp.dot(a, b, preferred_element_type=F32)


def split(a):
    high = a.astype(BF16)
    return high, (a - high.astype(F32)).astype(BF16)


def iota(shape, dim):
    return lax.broadcasted_iota(jnp.int32, shape, dim)


def kernel(
    tile_hbm,
    block_hbm,
    owner_hbm,
    row_hbm,
    atm_hbm,
    wet_hbm,
    kappa_hbm,
    w_hbm,
    ocean_hbm,
    vert_hbm,
    ocean_out,
    atm_out,
    tile_s,
    block_s,
    owner_ref,
    row_ref,
    block_ref,
    atm_ref,
    wet_ref,
    kappa_ref,
    atm_held,
    weights,
    weights_t,
    planes,
    vert,
    gain,
    first,
    flux,
    contrib,
    perm_t,
    row_held,
    row_out,
    row_mid,
    row_next,
    row_in,
    send_f,
    recv_f,
    send_w,
    recv_w,
    send_1,
    recv_1,
    send_2,
    recv_2,
    forcing,
    faces,
    edge_x,
    halo_x,
    edge_y,
    halo_y,
    sides_y,
    coef_x,
    coef_hx,
    coef_y,
    coef_hy,
    picks,
    back,
    load_sem,
    out_sem,
    send_sem,
    recv_sem,
    halo_ss,
    halo_rs,
    row_ss,
    row_rs,
    ready,
):
    gx, gy = lax.axis_index("gx"), lax.axis_index("gy")
    me = gx * 8 + gy
    at_y = [((gx // 4 + d) % 4) * 4 for d in range(4)]
    at_x = [(gx % 4 + d) % 4 for d in range(4)]
    at_z = [((gy // 2 + d) % 4) * 2 for d in range(4)]
    at_c = [(gy % 2 + d) % 2 for d in range(2)]

    loads = [
        pltpu.make_async_copy(source, target, load_sem.at[i])
        for i, (source, target) in enumerate(
            (
                (owner_hbm, owner_ref),
                (row_hbm, row_ref),
                (atm_hbm, atm_ref),
                (w_hbm, weights),
                (tile_hbm, tile_s),
                (block_hbm, block_s),
                (block_hbm, block_ref),
                (wet_hbm, wet_ref),
                (kappa_hbm, kappa_ref),
                (vert_hbm, vert),
                (ocean_hbm, planes),
            )
        )
    ]
    for copy in loads:
        copy.start()

    barrier = pltpu.get_barrier_semaphore()
    for r in range(1, 16):
        pl.semaphore_signal(barrier, inc=1, device_id=((gx + r) % 16, gy), device_id_type=MESH)
    for r in range(1, 8):
        pl.semaphore_signal(barrier, inc=1, device_id=(gx, (gy + r) % 8), device_id_type=MESH)

    def send_all(number, source, target, pitch, rows, steps, own):
        def block(ref, d):
            return ref.at[pl.ds(pl.multiple_of(d * pitch, 8), rows), :]

        if own:
            pltpu.make_async_copy(block(source, me), block(target, me), recv_sem.at[number]).start()
        for dy, dx, dz, dc in steps:
            tx, ty = at_y[dy] + at_x[dx], at_z[dz] + at_c[dc]
            pltpu.make_async_remote_copy(
                src_ref=block(source, tx * 8 + ty),
                dst_ref=block(target, me),
                send_sem=send_sem.at[number],
                recv_sem=recv_sem.at[number],
                device_id=(tx, ty),
                device_id_type=MESH,
            ).start()

    def wait_bytes(ref, sem):
        pltpu.make_async_copy(ref, ref, sem).wait()

    loads[2].wait()
    a = [atm_ref[i : i + 1, :] for i in range(6)]
    speed = jnp.sqrt(a[0] * a[0] + a[1] * a[1] + 0.25)
    rows4 = [
        0.5 * speed * (a[2] - a[5]),
        a[4] - 0.3 * speed * a[3],
        0.2 * speed * a[0],
        0.2 * speed * a[1],
    ]
    blank = jnp.zeros((12, 128), F32)
    for b in range(48):
        flux[b] = jnp.concatenate(
            [v[:, b * 128 : b * 128 + 128] for v in rows4] + [blank], axis=0
        ).astype(BF16)

    loads[0].wait()
    loads[1].wait()
    hit = (iota((128, 256), 0) == owner_ref[...]).astype(F32)
    before = (iota((256, 256), 0) < iota((256, 256), 1)).astype(BF16)
    rank = dot(hit.astype(BF16), before)
    perm = [jnp.where(rank == float(r), hit, 0.0) for r in range(4)]
    rows_f = row_ref[...].astype(F32) + 1.0
    lane128 = iota((128, 128), 1)
    row_msg = jnp.zeros((128, 128), F32)
    for r in range(4):
        at = jnp.sum(perm[r] * rows_f, axis=1, keepdims=True) - 1.0
        row_msg = jnp.where(lane128 == r, at, row_msg)
        perm_t[:, r * 128 : r * 128 + 128] = jnp.transpose(perm[r]).astype(BF16)
    row_held[...] = row_msg
    for t in range(8):
        row_out[t] = row_held[pl.ds(t, 16, stride=8), :]

    loads[7].wait()
    loads[8].wait()
    wet = wet_ref[...].astype(F32)
    kappa = kappa_ref[...]
    row8 = iota((8, 128), 0)
    for side, r in ((0, 0), (1, 63)):
        coef_x[side] = jnp.where(row8 == 0, kappa[r : r + 1, :], wet[r : r + 1, :])
    lane = iota((64, 128), 1)
    low, high = lane == 0, lane == 127
    packed = jnp.where(low, pltpu.roll(kappa, 1, 1), pltpu.roll(wet, 2, 1))
    packed = jnp.where(lane == 2, pltpu.roll(kappa, 2, 1), packed)
    coef_y[...] = jnp.where(lane == 3, pltpu.roll(wet, 3, 1), packed)

    for i in (3, 4, 5):
        loads[i].wait()

    def forward(g, _):
        for i in range(16):
            p = g * 16 + i
            out = dot(flux[block_s[0, p]], weights[tile_s[0, p]])
            contrib[pl.ds(pl.multiple_of(p * 8, 8), 8), :] = out[0:8]
        return 0

    lax.fori_loop(0, 6, forward, 0)

    pl.semaphore_wait(barrier, 22)
    for r in range(1, 8):
        pl.semaphore_signal(ready, inc=1, device_id=(gx, (gy + r) % 8), device_id_type=MESH)
    pltpu.make_async_copy(row_out.at[gy], row_mid.at[gy], row_rs.at[0]).start()
    for r in range(1, 8):
        t = (gy + r) % 8
        pltpu.make_async_remote_copy(
            src_ref=row_out.at[t],
            dst_ref=row_mid.at[gy],
            send_sem=row_ss.at[0],
            recv_sem=row_rs.at[0],
            device_id=(gx, t),
            device_id_type=MESH,
        ).start()

    lax.fori_loop(6, 16, forward, 0)

    wait_bytes(row_mid, row_rs.at[0])
    mid = row_mid[...].reshape(128, 128)
    row_held[...] = mid
    for t in range(16):
        row_next[t] = row_held[pl.ds(t, 8, stride=16), :]
    pltpu.make_async_copy(row_next.at[gx], row_in.at[gx], row_rs.at[1]).start()
    for r in range(1, 16):
        t = (gx + r) % 16
        pltpu.make_async_remote_copy(
            src_ref=row_next.at[t],
            dst_ref=row_in.at[gx],
            send_sem=row_ss.at[1],
            recv_sem=row_rs.at[1],
            device_id=(t, gy),
            device_id_type=MESH,
        ).start()

    part_h, part_l = split(
        jnp.concatenate([contrib[pl.ds(c, 256, stride=8), :] for c in range(4)], axis=1)
    )
    for r in range(4):
        pick = perm[r].astype(BF16)
        out = dot(pick, part_h) + dot(pick, part_l)
        for c in range(4):
            send_f[pl.ds(c * 4 + r, 128, stride=16), :] = out[:, c * 128 : c * 128 + 128]

    near = [((gx + 15) % 16, gy), ((gx + 1) % 16, gy), (gx, (gy + 7) % 8), (gx, (gy + 1) % 8)]

    def swap(number, sources, targets):
        copies = []
        for side in range(4):
            copies.append(
                pltpu.make_async_remote_copy(
                    src_ref=sources[side],
                    dst_ref=targets[side ^ 1],
                    send_sem=halo_ss.at[number, side],
                    recv_sem=halo_rs.at[number, side ^ 1],
                    device_id=near[side],
                    device_id_type=MESH,
                )
            )
        for copy in copies:
            copy.start()
        return copies

    pl.semaphore_wait(ready, 7)
    send_all(0, send_f, recv_f, 16, 16, ORDER, True)
    coef_copies = swap(
        0,
        [coef_x.at[0], coef_x.at[1], coef_y, coef_y],
        [coef_hx.at[0], coef_hx.at[1], coef_hy.at[0], coef_hy.at[1]],
    )

    wait_bytes(row_in, row_rs.at[1])
    rows_in = row_in[...].reshape(128, 128)
    rows_t = jnp.transpose(rows_in)
    x64 = iota((64, 128), 0).astype(F32)
    place = jnp.concatenate([(x64 == rows_t[r : r + 1, :]).astype(F32) for r in range(4)], axis=1)
    place = place.astype(BF16)
    twice = (lane128 % 64).astype(F32)
    fetch = [(rows_in[:, r : r + 1] == twice).astype(F32).astype(BF16) for r in range(4)]

    def give_back(source, target, pitch):
        parts = [split(v) for v in source]
        stacked = jnp.concatenate([jnp.concatenate([h, l], axis=0) for h, l in parts], axis=1)
        for r in range(4):
            out = dot(fetch[r], stacked)
            for c in range(len(source)):
                target[pl.ds(c * 4 + r, 128, stride=pitch), :] = out[:, c * 128 : c * 128 + 128]

    give_back([wet], send_w, 8)
    send_all(1, send_w, recv_w, 8, 4, ORDER, True)

    loads[9].wait()
    loads[10].wait()

    def solve(i, _):
        def at(level):
            return pl.ds(pl.multiple_of(level * 64 + i * 8, 8), 8)

        kap = [vert[at(l), :] for l in range(16)]
        face = [0.5 * (kap[l] + kap[l + 1]) for l in range(15)]
        inv, upper = [], []
        for l in range(16):
            above = face[l - 1] if l > 0 else 0.0
            below = face[l] if l < 15 else 0.0
            diagonal = 1.0 + above + below
            inv.append(1.0 / (diagonal + above * upper[-1] if l > 0 else diagonal))
            upper.append(-below * inv[-1])
        for field in range(5):
            held = []
            for l in range(16):
                if field < 4:
                    value = planes[at(field * 16 + l), :]
                    value = value + face[l - 1] * held[-1] if l > 0 else value
                    held.append(value * inv[l])
                else:
                    held.append(face[l - 1] * held[-1] * inv[l] if l > 0 else inv[l])
            value = held[15]
            for l in range(15, -1, -1):
                value = held[l] - upper[l] * value if l < 15 else value
                if field < 4:
                    planes[at(field * 16 + l), :] = value
                else:
                    gain[at(l), :] = value
        return 0

    lax.fori_loop(0, 8, solve, 0)

    for copy in coef_copies:
        copy.wait()

    def edge_row(side, row, there):
        return jnp.where(there, coef_hx[side, row : row + 1, :], 0.0)

    row64 = iota((64, 128), 0)
    sides = []
    for side, shift, there, edge in (
        (0, 1, gx > 0, row64 == 0),
        (1, 63, gx < 15, row64 == 63),
    ):
        sides.append(
            [
                jnp.where(edge, edge_row(side, v, there), pltpu.roll(field, shift, 0))
                for v, field in enumerate((kappa, wet))
            ]
        )
    for side, shift, there, edge, lanes in (
        (0, 1, gy > 0, low, (0, 1)),
        (1, 127, gy < 7, high, (2, 3)),
    ):
        got = jnp.where(there, coef_hy[side], 0.0)
        goal = 0 if side == 0 else 127
        sides.append(
            [
                jnp.where(edge, pltpu.roll(got, (goal - lanes[v]) % 128, 1), pltpu.roll(field, shift, 1))
                for v, field in enumerate((kappa, wet))
            ]
        )
    for n, (kappa_n, wet_n) in enumerate(sides):
        faces[n] = 0.25 * (kappa + kappa_n) * wet * wet_n

    wait_bytes(recv_f, recv_sem.at[0])
    for c in range(4):
        got = jnp.concatenate(
            [recv_f[pl.ds(c * 4 + r, 128, stride=16), :] for r in range(4)], axis=0
        )
        got_h, got_l = split(got)
        forcing[c] = (dot(place, got_h) + dot(place, got_l)) * wet

    def mix_tracers(l, _):
        response = gain[pl.ds(pl.multiple_of(l * 64, 64), 64), :]
        for c in range(2):
            at = pl.ds(pl.multiple_of(c * 1024 + l * 64, 64), 64)
            planes[at, :] = planes[at, :] + response * forcing[c]
        return 0

    lax.fori_loop(0, 16, mix_tracers, 0)

    pair = lane // 2

    def send_edges(number, source):
        edge_x[number, 0] = source[pl.ds(0, 32, stride=64), :]
        edge_x[number, 1] = source[pl.ds(63, 32, stride=64), :]

        def pack(k, held):
            plane = source[pl.ds(pl.multiple_of(k * 64, 64), 64), :]
            return jnp.where(pair == k, pltpu.roll(plane, 2 * k + 1, 1), held)

        edge_y[number] = lax.fori_loop(0, 32, pack, jnp.zeros((64, 128), F32), unroll=8)
        return swap(
            1 + number,
            [edge_x.at[number, 0], edge_x.at[number, 1], edge_y.at[number], edge_y.at[number]],
            [halo_x.at[number, 0], halo_x.at[number, 1], halo_y.at[number, 0], halo_y.at[number, 1]],
        )

    def join_sides(number):
        left, right = halo_y[number, 0], halo_y[number, 1]
        sides_y[number] = jnp.where(lane % 2 == 1, pltpu.roll(left, 1, 1), pltpu.roll(right, 127, 1))

    def diffuse(number, source, target, k):
        at = pl.ds(pl.multiple_of(k * 64, 64), 64)
        q = source[at, :]
        up = jnp.where(row64 == 0, halo_x[number, 0, pl.ds(k, 1), :], pltpu.roll(q, 1, 0))
        down = jnp.where(row64 == 63, halo_x[number, 1, pl.ds(k, 1), :], pltpu.roll(q, 63, 0))
        beside = pltpu.roll(sides_y[number], 127 - 2 * k, 1)
        left = jnp.where(low, beside, pltpu.roll(q, 1, 1))
        right = jnp.where(high, beside, pltpu.roll(q, 127, 1))
        total = q
        for n, other in enumerate((up, down, left, right)):
            total = total + faces[n] * (other - q)
        target[at, :] = total

    copies_1 = send_edges(0, planes)
    response = gain[0:64, :]
    give_back(
        [(planes[c * 1024 : c * 1024 + 64, :] + response * forcing[c]) * wet for c in (2, 3)],
        send_1,
        8,
    )
    send_all(2, send_1, recv_1, 8, 8, ORDER[:64], True)
    for copy in copies_1:
        copy.wait()
    join_sides(0)

    def pass_1(k, _):
        diffuse(0, planes, first, k)
        return 0

    lax.fori_loop(0, 32, pass_1, 0, unroll=4)
    copies_2 = send_edges(1, first)
    send_all(2, send_1, recv_1, 8, 8, ORDER[64:], False)
    for copy in copies_2:
        copy.wait()
    join_sides(1)
    diffuse(1, first, planes, 0)
    diffuse(1, first, planes, 16)
    give_back([planes[c * 1024 : c * 1024 + 64, :] * wet for c in (0, 1)], send_2, 8)
    send_all(3, send_2, recv_2, 8, 8, ORDER, True)

    def turn(t, _):
        weights_t[t] = jnp.transpose(weights[t])
        return 0

    lax.fori_loop(0, 128, turn, 0, unroll=8)

    def pass_2(l, _):
        diffuse(1, first, planes, l)
        diffuse(1, first, planes, l + 16)
        return 0

    lax.fori_loop(1, 16, pass_2, 0, unroll=3)

    def mix_flow(l, _):
        response = gain[pl.ds(pl.multiple_of(l * 64, 64), 64), :]
        for c in (2, 3):
            at = pl.ds(pl.multiple_of(c * 1024 + l * 64, 64), 64)
            planes[at, :] = planes[at, :] + response * forcing[c]
        return 0

    lax.fori_loop(0, 16, mix_flow, 0)
    store = pltpu.make_async_copy(planes, ocean_out, out_sem.at[0])
    store.start()


    def take(source, pitch, c, plane):
        got = jnp.concatenate(
            [source[pl.ds(c * 4 + r, 128, stride=pitch), :] for r in range(4)], axis=0
        )
        for half, part in enumerate(split(got)):
            picks[pl.ds(half * 8 + plane, 256, stride=16), :] = dot(perm_t[...], part)

    wait_bytes(recv_w.at[pl.ds(0, 512), :], recv_sem.at[1])
    take(recv_w, 8, 0, 4)
    wait_bytes(recv_1, recv_sem.at[2])
    for c in range(2):
        take(recv_1, 8, c, c + 2)
    wait_bytes(recv_2, recv_sem.at[3])
    for c in range(2):
        take(recv_2, 8, c, c)

    def backward(g, _):
        for i in range(16):
            p = g * 16 + i
            rows = picks[pl.ds(pl.multiple_of(p * 16, 16), 16), :].astype(BF16)
            out = dot(rows, weights_t[tile_s[0, p]])
            back[pl.ds(pl.multiple_of(p * 8, 8), 8), :] = out[0:8] + out[8:16]
        return 0

    lax.fori_loop(0, 16, backward, 0)

    loads[6].wait()
    of_block = iota((192, 256), 0) // 4 == block_ref[...]
    plane_of = iota((192, 256), 0) % 4
    num = jnp.zeros((192, 128), F32)
    for c in range(4):
        member = jnp.where(of_block & (plane_of == c), 1.0, 0.0).astype(BF16)
        for part in split(back[pl.ds(c, 256, stride=8), :]):
            num = num + dot(member, part)
    den = jnp.zeros((192, 128), F32)
    member = jnp.where(of_block, 1.0, 0.0).astype(BF16)
    for part in split(back[pl.ds(4, 256, stride=8), :]):
        den = den + dot(member, part)
    atm_held[...] = num / jnp.maximum(den, 0.1)
    store_atm = pltpu.make_async_copy(atm_held, atm_out, out_sem.at[1])
    store_atm.start()

    wait_bytes(send_f.at[pl.ds(0, 127 * 16), :], send_sem.at[0])
    wait_bytes(row_out.at[pl.ds(0, 7)], row_ss.at[0])
    wait_bytes(row_next.at[pl.ds(0, 15)], row_ss.at[1])
    wait_bytes(send_w.at[pl.ds(0, 127 * 4), :], send_sem.at[1])
    wait_bytes(send_1.at[pl.ds(0, 127 * 8), :], send_sem.at[2])
    wait_bytes(send_2.at[pl.ds(0, 127 * 8), :], send_sem.at[3])
    store.wait()
    store_atm.wait()


def hand_over(ocean_in, atm_in, ocean_out, atm_out, held, atm_held, atm_done, in_sem, out_sem):
    atm_load = pltpu.make_async_copy(atm_in, atm_held, in_sem.at[4])
    atm_load.start()
    parts = [pl.ds(i * 1024, 1024) for i in range(4)]
    loads = [
        pltpu.make_async_copy(ocean_in.at[at, :], held.at[at, :], in_sem.at[i])
        for i, at in enumerate(parts)
    ]
    stores = [
        pltpu.make_async_copy(held.at[at, :], ocean_out.at[at, :], out_sem.at[i])
        for i, at in enumerate(parts)
    ]
    stores.append(pltpu.make_async_copy(atm_done, atm_out, out_sem.at[4]))
    for copy in loads:
        copy.start()
    atm_load.wait()
    for b in range(48):
        atm_done[:, b * 128 : b * 128 + 128] = atm_held[b * 4 : b * 4 + 4, :]
    stores[4].start()
    for load, store in zip(loads, stores):
        load.wait()
        store.start()
    for copy in stores:
        copy.wait()


def local(
    atm_state,
    pair_block,
    pair_owner,
    pair_row,
    pair_tile,
    remap_weight,
    wet_mask,
    ocean_state,
    vert_kappa,
    horiz_kappa,
):
    hbm = pl.BlockSpec(memory_space=pl.ANY)
    dma = pltpu.SemaphoreType.DMA

    def buffer(*shape, dtype=F32):
        return pltpu.VMEM(shape, dtype)

    ocean, atm = pl.pallas_call(
        kernel,
        out_shape=(
            jax.ShapeDtypeStruct((4096, 128), F32),
            jax.ShapeDtypeStruct((192, 128), F32),
        ),
        in_specs=[hbm] * 10,
        out_specs=(hbm, hbm),
        scratch_shapes=[
            pltpu.SMEM((1, 256), jnp.int32),
            pltpu.SMEM((1, 256), jnp.int32),
            buffer(1, 256, dtype=jnp.int32),
            buffer(1, 256, dtype=jnp.int32),
            buffer(1, 256, dtype=jnp.int32),
            buffer(6, 6144),
            buffer(64, 128, dtype=jnp.int32),
            buffer(64, 128),
            buffer(192, 128),
            buffer(128, 128, 128, dtype=BF16),
            buffer(128, 128, 128, dtype=BF16),
            buffer(4096, 128),
            buffer(1024, 128),
            buffer(1024, 128),
            buffer(2048, 128),
            buffer(48, 16, 128, dtype=BF16),
            buffer(2048, 128),
            buffer(256, 512, dtype=BF16),
            buffer(128, 128),
            buffer(8, 16, 128),
            buffer(8, 16, 128),
            buffer(16, 8, 128),
            buffer(16, 8, 128),
            buffer(2048, 128),
            buffer(2048, 128),
            buffer(1024, 128),
            buffer(1024, 128),
            buffer(1024, 128),
            buffer(1024, 128),
            buffer(1024, 128),
            buffer(1024, 128),
            buffer(4, 64, 128),
            buffer(4, 64, 128),
            buffer(2, 2, 32, 128),
            buffer(2, 2, 32, 128),
            buffer(2, 64, 128),
            buffer(2, 2, 64, 128),
            buffer(2, 64, 128),
            buffer(2, 8, 128),
            buffer(2, 8, 128),
            buffer(64, 128),
            buffer(2, 64, 128),
            buffer(4096, 128),
            buffer(2048, 128),
            dma((11,)),
            dma((2,)),
            dma((4,)),
            dma((4,)),
            dma((3, 4)),
            dma((3, 4)),
            dma((2,)),
            dma((2,)),
            pltpu.SemaphoreType.REGULAR,
        ],
        compiler_params=pltpu.CompilerParams(
            collective_id=0, has_side_effects=True, vmem_limit_bytes=63 << 20
        ),
        name="couple",
    )(
        pair_tile.reshape(1, 256),
        pair_block.reshape(1, 256),
        pair_owner.reshape(1, 256),
        pair_row.reshape(1, 256),
        atm_state,
        wet_mask,
        horiz_kappa,
        remap_weight,
        ocean_state.reshape(4096, 128),
        vert_kappa.reshape(1024, 128),
    )
    ocean_next, atm_surface = pl.pallas_call(
        hand_over,
        out_shape=(
            jax.ShapeDtypeStruct((4096, 128), F32),
            jax.ShapeDtypeStruct((4, 6144), F32),
        ),
        in_specs=[hbm, hbm],
        out_specs=(hbm, hbm),
        scratch_shapes=[
            buffer(4096, 128),
            buffer(192, 128),
            buffer(4, 6144),
            dma((5,)),
            dma((5,)),
        ],
        compiler_params=pltpu.CompilerParams(vmem_limit_bytes=63 << 20),
        name="hand_over",
    )(ocean, atm)
    return (ocean_next.reshape(4, 16, 64, 128), atm_surface)


def solution(mesh):
    placed = (
        P(None, ("gx", "gy")),
        P(("gx", "gy")),
        P(("gx", "gy"), None),
        P(("gx", "gy")),
        P(("gx", "gy")),
        P(("gx", "gy"), None, None),
        P("gx", "gy"),
        P(None, None, "gx", "gy"),
        P(None, "gx", "gy"),
        P("gx", "gy"),
    )
    return jax.shard_map(
        local,
        mesh=mesh,
        in_specs=placed,
        out_specs=(P(None, None, "gx", "gy"), P(None, ("gx", "gy"))),
        check_vma=False,
    )
```

```python
import itertools
import random

import jax
import jax.numpy as jnp
from jax import lax
from jax.experimental import pallas as pl
from jax.experimental.pallas import tpu as pltpu
from jax.sharding import PartitionSpec as P

MESH = pl.DeviceIdType.MESH
F32 = jnp.float32
BF16 = jnp.bfloat16


def hops(step):
    return sum(min(v, 4 - v) for v in step[:3])


def send_order():
    steps = [s for s in itertools.product(range(4), range(4), range(4), range(2)) if any(s)]
    random.Random(0).shuffle(steps)
    return sorted(steps, key=lambda s: -hops(s))


ORDER = send_order()


def dot(a, b):
    return jnp.dot(a, b, preferred_element_type=F32)


def split(a):
    high = a.astype(BF16)
    return high, (a - high.astype(F32)).astype(BF16)


def iota(shape, dim):
    return lax.broadcasted_iota(jnp.int32, shape, dim)


def kernel(
    tile_hbm,
    block_hbm,
    owner_hbm,
    row_hbm,
    atm_hbm,
    wet_hbm,
    kappa_hbm,
    w_hbm,
    ocean_hbm,
    vert_hbm,
    ocean_out,
    atm_out,
    tile_s,
    block_s,
    owner_ref,
    row_ref,
    block_ref,
    atm_ref,
    wet_ref,
    kappa_ref,
    atm_held,
    weights,
    weights_t,
    planes,
    vert,
    gain,
    first,
    flux,
    contrib,
    perm_t,
    row_held,
    row_out,
    row_mid,
    row_next,
    row_in,
    send_f,
    recv_f,
    send_w,
    recv_w,
    send_1,
    recv_1,
    send_2,
    recv_2,
    forcing,
    faces,
    edge_x,
    halo_x,
    edge_y,
    halo_y,
    sides_y,
    coef_x,
    coef_hx,
    coef_y,
    coef_hy,
    picks,
    back,
    load_sem,
    out_sem,
    send_sem,
    recv_sem,
    halo_ss,
    halo_rs,
    row_ss,
    row_rs,
    ready,
):
    gx, gy = lax.axis_index("gx"), lax.axis_index("gy")
    me = gx * 8 + gy
    way = 1 - 2 * (gy % 2)
    at_y = [((gx // 4 + 4 + way * d) % 4) * 4 for d in range(4)]
    at_x = [(gx % 4 + 4 + way * d) % 4 for d in range(4)]
    at_z = [((gy // 2 + 4 + way * d) % 4) * 2 for d in range(4)]
    at_c = [(gy % 2 + d) % 2 for d in range(2)]

    loads = [
        pltpu.make_async_copy(source, target, load_sem.at[i])
        for i, (source, target) in enumerate(
            (
                (owner_hbm, owner_ref),
                (row_hbm, row_ref),
                (atm_hbm, atm_ref),
                (w_hbm, weights),
                (tile_hbm, tile_s),
                (block_hbm, block_s),
                (block_hbm, block_ref),
                (wet_hbm, wet_ref),
                (kappa_hbm, kappa_ref),
                (vert_hbm, vert),
                (ocean_hbm, planes),
            )
        )
    ]
    for copy in loads:
        copy.start()

    barrier = pltpu.get_barrier_semaphore()
    for r in range(1, 16):
        pl.semaphore_signal(barrier, inc=1, device_id=((gx + r) % 16, gy), device_id_type=MESH)
    for r in range(1, 8):
        pl.semaphore_signal(barrier, inc=1, device_id=(gx, (gy + r) % 8), device_id_type=MESH)

    def send_all(number, source, target, pitch, rows, steps, own):
        def block(ref, d):
            return ref.at[pl.ds(pl.multiple_of(d * pitch, 8), rows), :]

        if own:
            pltpu.make_async_copy(block(source, me), block(target, me), recv_sem.at[number]).start()
        for dy, dx, dz, dc in steps:
            tx, ty = at_y[dy] + at_x[dx], at_z[dz] + at_c[dc]
            pltpu.make_async_remote_copy(
                src_ref=block(source, tx * 8 + ty),
                dst_ref=block(target, me),
                send_sem=send_sem.at[number],
                recv_sem=recv_sem.at[number],
                device_id=(tx, ty),
                device_id_type=MESH,
            ).start()

    def wait_bytes(ref, sem):
        pltpu.make_async_copy(ref, ref, sem).wait()

    loads[2].wait()
    a = [atm_ref[i : i + 1, :] for i in range(6)]
    speed = jnp.sqrt(a[0] * a[0] + a[1] * a[1] + 0.25)
    rows4 = [
        0.5 * speed * (a[2] - a[5]),
        a[4] - 0.3 * speed * a[3],
        0.2 * speed * a[0],
        0.2 * speed * a[1],
    ]
    blank = jnp.zeros((12, 128), F32)
    for b in range(48):
        flux[b] = jnp.concatenate(
            [v[:, b * 128 : b * 128 + 128] for v in rows4] + [blank], axis=0
        ).astype(BF16)

    loads[0].wait()
    loads[1].wait()
    hit = (iota((128, 256), 0) == owner_ref[...]).astype(F32)
    before = (iota((256, 256), 0) < iota((256, 256), 1)).astype(BF16)
    rank = dot(hit.astype(BF16), before)
    perm = [jnp.where(rank == float(r), hit, 0.0) for r in range(4)]
    rows_f = row_ref[...].astype(F32) + 1.0
    lane128 = iota((128, 128), 1)
    row_msg = jnp.zeros((128, 128), F32)
    for r in range(4):
        at = jnp.sum(perm[r] * rows_f, axis=1, keepdims=True) - 1.0
        row_msg = jnp.where(lane128 == r, at, row_msg)
        perm_t[:, r * 128 : r * 128 + 128] = jnp.transpose(perm[r]).astype(BF16)
    row_held[...] = row_msg
    for t in range(8):
        row_out[t] = row_held[pl.ds(t, 16, stride=8), :]

    loads[7].wait()
    loads[8].wait()
    wet = wet_ref[...].astype(F32)
    kappa = kappa_ref[...]
    row8 = iota((8, 128), 0)
    for side, r in ((0, 0), (1, 63)):
        coef_x[side] = jnp.where(row8 == 0, kappa[r : r + 1, :], wet[r : r + 1, :])
    lane = iota((64, 128), 1)
    low, high = lane == 0, lane == 127
    packed = jnp.where(low, pltpu.roll(kappa, 1, 1), pltpu.roll(wet, 2, 1))
    packed = jnp.where(lane == 2, pltpu.roll(kappa, 2, 1), packed)
    coef_y[...] = jnp.where(lane == 3, pltpu.roll(wet, 3, 1), packed)

    for i in (3, 4, 5):
        loads[i].wait()

    def forward(g, _):
        for i in range(16):
            p = g * 16 + i
            out = dot(flux[block_s[0, p]], weights[tile_s[0, p]])
            contrib[pl.ds(pl.multiple_of(p * 8, 8), 8), :] = out[0:8]
        return 0

    lax.fori_loop(0, 1, forward, 0)

    pl.semaphore_wait(barrier, 22)
    for r in range(1, 8):
        pl.semaphore_signal(ready, inc=1, device_id=(gx, (gy + r) % 8), device_id_type=MESH)
    pltpu.make_async_copy(row_out.at[gy], row_mid.at[gy], row_rs.at[0]).start()
    for r in range(1, 8):
        t = (gy + r) % 8
        pltpu.make_async_remote_copy(
            src_ref=row_out.at[t],
            dst_ref=row_mid.at[gy],
            send_sem=row_ss.at[0],
            recv_sem=row_rs.at[0],
            device_id=(gx, t),
            device_id_type=MESH,
        ).start()

    lax.fori_loop(1, 16, forward, 0)

    part_h, part_l = split(
        jnp.concatenate([contrib[pl.ds(c, 256, stride=8), :] for c in range(4)], axis=1)
    )
    for r in range(4):
        pick = perm[r].astype(BF16)
        out = dot(pick, part_h) + dot(pick, part_l)
        for c in range(4):
            send_f[pl.ds(c * 4 + r, 128, stride=16), :] = out[:, c * 128 : c * 128 + 128]

    wait_bytes(row_mid, row_rs.at[0])
    mid = row_mid[...].reshape(128, 128)
    row_held[...] = mid
    for t in range(16):
        row_next[t] = row_held[pl.ds(t, 8, stride=16), :]
    pltpu.make_async_copy(row_next.at[gx], row_in.at[gx], row_rs.at[1]).start()
    for r in range(1, 16):
        t = (gx + r) % 16
        pltpu.make_async_remote_copy(
            src_ref=row_next.at[t],
            dst_ref=row_in.at[gx],
            send_sem=row_ss.at[1],
            recv_sem=row_rs.at[1],
            device_id=(t, gy),
            device_id_type=MESH,
        ).start()

    near = [((gx + 15) % 16, gy), ((gx + 1) % 16, gy), (gx, (gy + 7) % 8), (gx, (gy + 1) % 8)]

    def swap(number, sources, targets):
        copies = []
        for side in range(4):
            copies.append(
                pltpu.make_async_remote_copy(
                    src_ref=sources[side],
                    dst_ref=targets[side ^ 1],
                    send_sem=halo_ss.at[number, side],
                    recv_sem=halo_rs.at[number, side ^ 1],
                    device_id=near[side],
                    device_id_type=MESH,
                )
            )
        for copy in copies:
            copy.start()
        return copies

    pl.semaphore_wait(ready, 7)
    send_all(0, send_f, recv_f, 16, 16, ORDER, True)
    coef_copies = swap(
        0,
        [coef_x.at[0], coef_x.at[1], coef_y, coef_y],
        [coef_hx.at[0], coef_hx.at[1], coef_hy.at[0], coef_hy.at[1]],
    )

    wait_bytes(row_in, row_rs.at[1])
    rows_in = row_in[...].reshape(128, 128)
    rows_t = jnp.transpose(rows_in)
    x64 = iota((64, 128), 0).astype(F32)
    place = jnp.concatenate([(x64 == rows_t[r : r + 1, :]).astype(F32) for r in range(4)], axis=1)
    place = place.astype(BF16)
    twice = (lane128 % 64).astype(F32)
    fetch = [(rows_in[:, r : r + 1] == twice).astype(F32).astype(BF16) for r in range(4)]

    def give_back(source, target, pitch):
        parts = [split(v) for v in source]
        stacked = jnp.concatenate([jnp.concatenate([h, l], axis=0) for h, l in parts], axis=1)
        for r in range(4):
            out = dot(fetch[r], stacked)
            for c in range(len(source)):
                target[pl.ds(c * 4 + r, 128, stride=pitch), :] = out[:, c * 128 : c * 128 + 128]

    give_back([wet], send_w, 8)
    send_all(1, send_w, recv_w, 8, 4, ORDER, True)

    loads[9].wait()
    loads[10].wait()

    def solve(i, _):
        def at(level):
            return pl.ds(pl.multiple_of(level * 64 + i * 8, 8), 8)

        kap = [vert[at(l), :] for l in range(16)]
        face = [0.5 * (kap[l] + kap[l + 1]) for l in range(15)]
        inv, upper = [], []
        for l in range(16):
            above = face[l - 1] if l > 0 else 0.0
            below = face[l] if l < 15 else 0.0
            diagonal = 1.0 + above + below
            inv.append(1.0 / (diagonal + above * upper[-1] if l > 0 else diagonal))
            upper.append(-below * inv[-1])
        for field in range(5):
            held = []
            for l in range(16):
                if field < 4:
                    value = planes[at(field * 16 + l), :]
                    value = value + face[l - 1] * held[-1] if l > 0 else value
                    held.append(value * inv[l])
                else:
                    held.append(face[l - 1] * held[-1] * inv[l] if l > 0 else inv[l])
            value = held[15]
            for l in range(15, -1, -1):
                value = held[l] - upper[l] * value if l < 15 else value
                if field < 4:
                    planes[at(field * 16 + l), :] = value
                else:
                    gain[at(l), :] = value
        return 0

    lax.fori_loop(0, 8, solve, 0)

    for copy in coef_copies:
        copy.wait()

    def edge_row(side, row, there):
        return jnp.where(there, coef_hx[side, row : row + 1, :], 0.0)

    row64 = iota((64, 128), 0)
    sides = []
    for side, shift, there, edge in (
        (0, 1, gx > 0, row64 == 0),
        (1, 63, gx < 15, row64 == 63),
    ):
        sides.append(
            [
                jnp.where(edge, edge_row(side, v, there), pltpu.roll(field, shift, 0))
                for v, field in enumerate((kappa, wet))
            ]
        )
    for side, shift, there, edge, lanes in (
        (0, 1, gy > 0, low, (0, 1)),
        (1, 127, gy < 7, high, (2, 3)),
    ):
        got = jnp.where(there, coef_hy[side], 0.0)
        goal = 0 if side == 0 else 127
        sides.append(
            [
                jnp.where(edge, pltpu.roll(got, (goal - lanes[v]) % 128, 1), pltpu.roll(field, shift, 1))
                for v, field in enumerate((kappa, wet))
            ]
        )
    for n, (kappa_n, wet_n) in enumerate(sides):
        faces[n] = 0.25 * (kappa + kappa_n) * wet * wet_n

    wait_bytes(recv_f, recv_sem.at[0])
    for c in range(4):
        got = jnp.concatenate(
            [recv_f[pl.ds(c * 4 + r, 128, stride=16), :] for r in range(4)], axis=0
        )
        got_h, got_l = split(got)
        forcing[c] = (dot(place, got_h) + dot(place, got_l)) * wet

    def mix_tracers(l, _):
        response = gain[pl.ds(pl.multiple_of(l * 64, 64), 64), :]
        for c in range(2):
            at = pl.ds(pl.multiple_of(c * 1024 + l * 64, 64), 64)
            planes[at, :] = planes[at, :] + response * forcing[c]
        return 0

    lax.fori_loop(0, 16, mix_tracers, 0)

    pair = lane // 2

    def send_edges(number, source):
        edge_x[number, 0] = source[pl.ds(0, 32, stride=64), :]
        edge_x[number, 1] = source[pl.ds(63, 32, stride=64), :]

        def pack(k, held):
            plane = source[pl.ds(pl.multiple_of(k * 64, 64), 64), :]
            return jnp.where(pair == k, pltpu.roll(plane, 2 * k + 1, 1), held)

        edge_y[number] = lax.fori_loop(0, 32, pack, jnp.zeros((64, 128), F32), unroll=8)
        return swap(
            1 + number,
            [edge_x.at[number, 0], edge_x.at[number, 1], edge_y.at[number], edge_y.at[number]],
            [halo_x.at[number, 0], halo_x.at[number, 1], halo_y.at[number, 0], halo_y.at[number, 1]],
        )

    def join_sides(number):
        left, right = halo_y[number, 0], halo_y[number, 1]
        sides_y[number] = jnp.where(lane % 2 == 1, pltpu.roll(left, 1, 1), pltpu.roll(right, 127, 1))

    def diffuse(number, source, target, k):
        at = pl.ds(pl.multiple_of(k * 64, 64), 64)
        q = source[at, :]
        up = jnp.where(row64 == 0, halo_x[number, 0, pl.ds(k, 1), :], pltpu.roll(q, 1, 0))
        down = jnp.where(row64 == 63, halo_x[number, 1, pl.ds(k, 1), :], pltpu.roll(q, 63, 0))
        beside = pltpu.roll(sides_y[number], 127 - 2 * k, 1)
        left = jnp.where(low, beside, pltpu.roll(q, 1, 1))
        right = jnp.where(high, beside, pltpu.roll(q, 127, 1))
        total = q
        for n, other in enumerate((up, down, left, right)):
            total = total + faces[n] * (other - q)
        target[at, :] = total

    copies_1 = send_edges(0, planes)
    response = gain[0:64, :]
    give_back(
        [(planes[c * 1024 : c * 1024 + 64, :] + response * forcing[c]) * wet for c in (2, 3)],
        send_1,
        8,
    )
    send_all(2, send_1, recv_1, 8, 8, ORDER[:64], True)
    for copy in copies_1:
        copy.wait()
    join_sides(0)

    def pass_1(k, _):
        diffuse(0, planes, first, k)
        return 0

    lax.fori_loop(0, 32, pass_1, 0, unroll=4)
    copies_2 = send_edges(1, first)
    send_all(2, send_1, recv_1, 8, 8, ORDER[64:], False)
    for copy in copies_2:
        copy.wait()
    join_sides(1)
    diffuse(1, first, planes, 0)
    diffuse(1, first, planes, 16)
    give_back([planes[c * 1024 : c * 1024 + 64, :] * wet for c in (0, 1)], send_2, 8)
    send_all(3, send_2, recv_2, 8, 8, ORDER, True)

    def turn(t, _):
        weights_t[t] = jnp.transpose(weights[t])
        return 0

    lax.fori_loop(0, 128, turn, 0, unroll=8)

    def pass_2(l, _):
        diffuse(1, first, planes, l)
        diffuse(1, first, planes, l + 16)
        return 0

    lax.fori_loop(1, 16, pass_2, 0, unroll=3)

    def mix_flow(l, _):
        response = gain[pl.ds(pl.multiple_of(l * 64, 64), 64), :]
        for c in (2, 3):
            at = pl.ds(pl.multiple_of(c * 1024 + l * 64, 64), 64)
            planes[at, :] = planes[at, :] + response * forcing[c]
        return 0

    lax.fori_loop(0, 16, mix_flow, 0)
    store = pltpu.make_async_copy(planes, ocean_out, out_sem.at[0])
    store.start()


    def take(source, pitch, c, plane):
        got = jnp.concatenate(
            [source[pl.ds(c * 4 + r, 128, stride=pitch), :] for r in range(4)], axis=0
        )
        for half, part in enumerate(split(got)):
            picks[pl.ds(half * 8 + plane, 256, stride=16), :] = dot(perm_t[...], part)

    wait_bytes(recv_w.at[pl.ds(0, 512), :], recv_sem.at[1])
    take(recv_w, 8, 0, 4)
    wait_bytes(recv_1, recv_sem.at[2])
    for c in range(2):
        take(recv_1, 8, c, c + 2)
    wait_bytes(recv_2, recv_sem.at[3])
    for c in range(2):
        take(recv_2, 8, c, c)

    def backward(g, _):
        for i in range(16):
            p = g * 16 + i
            rows = picks[pl.ds(pl.multiple_of(p * 16, 16), 16), :].astype(BF16)
            out = dot(rows, weights_t[tile_s[0, p]])
            back[pl.ds(pl.multiple_of(p * 8, 8), 8), :] = out[0:8] + out[8:16]
        return 0

    lax.fori_loop(0, 16, backward, 0)

    loads[6].wait()
    of_block = iota((192, 256), 0) // 4 == block_ref[...]
    plane_of = iota((192, 256), 0) % 4
    num = jnp.zeros((192, 128), F32)
    for c in range(4):
        member = jnp.where(of_block & (plane_of == c), 1.0, 0.0).astype(BF16)
        for part in split(back[pl.ds(c, 256, stride=8), :]):
            num = num + dot(member, part)
    den = jnp.zeros((192, 128), F32)
    member = jnp.where(of_block, 1.0, 0.0).astype(BF16)
    for part in split(back[pl.ds(4, 256, stride=8), :]):
        den = den + dot(member, part)
    atm_held[...] = num / jnp.maximum(den, 0.1)
    store_atm = pltpu.make_async_copy(atm_held, atm_out, out_sem.at[1])
    store_atm.start()

    wait_bytes(send_f.at[pl.ds(0, 127 * 16), :], send_sem.at[0])
    wait_bytes(row_out.at[pl.ds(0, 7)], row_ss.at[0])
    wait_bytes(row_next.at[pl.ds(0, 15)], row_ss.at[1])
    wait_bytes(send_w.at[pl.ds(0, 127 * 4), :], send_sem.at[1])
    wait_bytes(send_1.at[pl.ds(0, 127 * 8), :], send_sem.at[2])
    wait_bytes(send_2.at[pl.ds(0, 127 * 8), :], send_sem.at[3])
    store.wait()
    store_atm.wait()


def hand_over(ocean_in, atm_in, ocean_out, atm_out, held, atm_held, atm_done, in_sem, out_sem):
    atm_load = pltpu.make_async_copy(atm_in, atm_held, in_sem.at[4])
    atm_load.start()
    parts = [pl.ds(i * 1024, 1024) for i in range(4)]
    loads = [
        pltpu.make_async_copy(ocean_in.at[at, :], held.at[at, :], in_sem.at[i])
        for i, at in enumerate(parts)
    ]
    stores = [
        pltpu.make_async_copy(held.at[at, :], ocean_out.at[at, :], out_sem.at[i])
        for i, at in enumerate(parts)
    ]
    stores.append(pltpu.make_async_copy(atm_done, atm_out, out_sem.at[4]))
    for copy in loads:
        copy.start()
    atm_load.wait()
    for b in range(48):
        atm_done[:, b * 128 : b * 128 + 128] = atm_held[b * 4 : b * 4 + 4, :]
    stores[4].start()
    for load, store in zip(loads, stores):
        load.wait()
        store.start()
    for copy in stores:
        copy.wait()


def local(
    atm_state,
    pair_block,
    pair_owner,
    pair_row,
    pair_tile,
    remap_weight,
    wet_mask,
    ocean_state,
    vert_kappa,
    horiz_kappa,
):
    hbm = pl.BlockSpec(memory_space=pl.ANY)
    dma = pltpu.SemaphoreType.DMA

    def buffer(*shape, dtype=F32):
        return pltpu.VMEM(shape, dtype)

    ocean, atm = pl.pallas_call(
        kernel,
        out_shape=(
            jax.ShapeDtypeStruct((4096, 128), F32),
            jax.ShapeDtypeStruct((192, 128), F32),
        ),
        in_specs=[hbm] * 10,
        out_specs=(hbm, hbm),
        scratch_shapes=[
            pltpu.SMEM((1, 256), jnp.int32),
            pltpu.SMEM((1, 256), jnp.int32),
            buffer(1, 256, dtype=jnp.int32),
            buffer(1, 256, dtype=jnp.int32),
            buffer(1, 256, dtype=jnp.int32),
            buffer(6, 6144),
            buffer(64, 128, dtype=jnp.int32),
            buffer(64, 128),
            buffer(192, 128),
            buffer(128, 128, 128, dtype=BF16),
            buffer(128, 128, 128, dtype=BF16),
            buffer(4096, 128),
            buffer(1024, 128),
            buffer(1024, 128),
            buffer(2048, 128),
            buffer(48, 16, 128, dtype=BF16),
            buffer(2048, 128),
            buffer(256, 512, dtype=BF16),
            buffer(128, 128),
            buffer(8, 16, 128),
            buffer(8, 16, 128),
            buffer(16, 8, 128),
            buffer(16, 8, 128),
            buffer(2048, 128),
            buffer(2048, 128),
            buffer(1024, 128),
            buffer(1024, 128),
            buffer(1024, 128),
            buffer(1024, 128),
            buffer(1024, 128),
            buffer(1024, 128),
            buffer(4, 64, 128),
            buffer(4, 64, 128),
            buffer(2, 2, 32, 128),
            buffer(2, 2, 32, 128),
            buffer(2, 64, 128),
            buffer(2, 2, 64, 128),
            buffer(2, 64, 128),
            buffer(2, 8, 128),
            buffer(2, 8, 128),
            buffer(64, 128),
            buffer(2, 64, 128),
            buffer(4096, 128),
            buffer(2048, 128),
            dma((11,)),
            dma((2,)),
            dma((4,)),
            dma((4,)),
            dma((3, 4)),
            dma((3, 4)),
            dma((2,)),
            dma((2,)),
            pltpu.SemaphoreType.REGULAR,
        ],
        compiler_params=pltpu.CompilerParams(
            collective_id=0, has_side_effects=True, vmem_limit_bytes=63 << 20
        ),
        name="couple",
    )(
        pair_tile.reshape(1, 256),
        pair_block.reshape(1, 256),
        pair_owner.reshape(1, 256),
        pair_row.reshape(1, 256),
        atm_state,
        wet_mask,
        horiz_kappa,
        remap_weight,
        ocean_state.reshape(4096, 128),
        vert_kappa.reshape(1024, 128),
    )
    ocean_next, atm_surface = pl.pallas_call(
        hand_over,
        out_shape=(
            jax.ShapeDtypeStruct((4096, 128), F32),
            jax.ShapeDtypeStruct((4, 6144), F32),
        ),
        in_specs=[hbm, hbm],
        out_specs=(hbm, hbm),
        scratch_shapes=[
            buffer(4096, 128),
            buffer(192, 128),
            buffer(4, 6144),
            dma((5,)),
            dma((5,)),
        ],
        compiler_params=pltpu.CompilerParams(vmem_limit_bytes=63 << 20),
        name="hand_over",
    )(ocean, atm)
    return (ocean_next.reshape(4, 16, 64, 128), atm_surface)


def solution(mesh):
    placed = (
        P(None, ("gx", "gy")),
        P(("gx", "gy")),
        P(("gx", "gy"), None),
        P(("gx", "gy")),
        P(("gx", "gy")),
        P(("gx", "gy"), None, None),
        P("gx", "gy"),
        P(None, None, "gx", "gy"),
        P(None, "gx", "gy"),
        P("gx", "gy"),
    )
    return jax.shard_map(
        local,
        mesh=mesh,
        in_specs=placed,
        out_specs=(P(None, None, "gx", "gy"), P(None, ("gx", "gy"))),
        check_vma=False,
    )
```

```python
import itertools
import random

import jax
import jax.numpy as jnp
from jax import lax
from jax.experimental import pallas as pl
from jax.experimental.pallas import tpu as pltpu
from jax.sharding import PartitionSpec as P

MESH = pl.DeviceIdType.MESH
F32 = jnp.float32
BF16 = jnp.bfloat16


def hops(step):
    return sum(min(v, 4 - v) for v in step[:3])


def send_order():
    steps = [s for s in itertools.product(range(4), range(4), range(4), range(2)) if any(s)]
    random.Random(0).shuffle(steps)
    return sorted(steps, key=lambda s: -hops(s))


ORDER = send_order()


def dot(a, b):
    return jnp.dot(a, b, preferred_element_type=F32)


def split(a):
    high = a.astype(BF16)
    return high, (a - high.astype(F32)).astype(BF16)


def iota(shape, dim):
    return lax.broadcasted_iota(jnp.int32, shape, dim)


def kernel(
    tile_hbm,
    block_hbm,
    owner_hbm,
    row_hbm,
    atm_hbm,
    wet_hbm,
    kappa_hbm,
    w_hbm,
    ocean_hbm,
    vert_hbm,
    ocean_out,
    atm_out,
    tile_s,
    block_s,
    owner_ref,
    row_ref,
    block_ref,
    atm_ref,
    wet_ref,
    kappa_ref,
    atm_held,
    weights,
    weights_t,
    planes,
    vert,
    gain,
    first,
    flux,
    contrib,
    perm_t,
    row_held,
    row_out,
    row_mid,
    row_next,
    row_in,
    send_f,
    recv_f,
    send_w,
    recv_w,
    send_1,
    recv_1,
    send_2,
    recv_2,
    forcing,
    faces,
    edge_x,
    halo_x,
    edge_y,
    halo_y,
    sides_y,
    coef_x,
    coef_hx,
    coef_y,
    coef_hy,
    picks,
    back,
    load_sem,
    out_sem,
    send_sem,
    recv_sem,
    halo_ss,
    halo_rs,
    row_ss,
    row_rs,
    ready,
):
    gx, gy = lax.axis_index("gx"), lax.axis_index("gy")
    me = gx * 8 + gy
    way = 1 - 2 * (gy % 2)
    at_y = [((gx // 4 + 4 + way * d) % 4) * 4 for d in range(4)]
    at_x = [(gx % 4 + 4 + way * d) % 4 for d in range(4)]
    at_z = [((gy // 2 + 4 + way * d) % 4) * 2 for d in range(4)]
    at_c = [(gy % 2 + d) % 2 for d in range(2)]

    loads = [
        pltpu.make_async_copy(source, target, load_sem.at[i])
        for i, (source, target) in enumerate(
            (
                (owner_hbm, owner_ref),
                (row_hbm, row_ref),
                (atm_hbm, atm_ref),
                (w_hbm, weights),
                (tile_hbm, tile_s),
                (block_hbm, block_s),
                (block_hbm, block_ref),
                (wet_hbm, wet_ref),
                (kappa_hbm, kappa_ref),
                (vert_hbm, vert),
                (ocean_hbm, planes),
            )
        )
    ]
    for copy in loads:
        copy.start()

    barrier = pltpu.get_barrier_semaphore()
    for r in range(1, 16):
        pl.semaphore_signal(barrier, inc=1, device_id=((gx + r) % 16, gy), device_id_type=MESH)
    for r in range(1, 8):
        pl.semaphore_signal(barrier, inc=1, device_id=(gx, (gy + r) % 8), device_id_type=MESH)

    def send_all(number, source, target, pitch, rows, steps, own):
        def block(ref, d):
            return ref.at[pl.ds(pl.multiple_of(d * pitch, 8), rows), :]

        if own:
            pltpu.make_async_copy(block(source, me), block(target, me), recv_sem.at[number]).start()
        for dy, dx, dz, dc in steps:
            tx, ty = at_y[dy] + at_x[dx], at_z[dz] + at_c[dc]
            pltpu.make_async_remote_copy(
                src_ref=block(source, tx * 8 + ty),
                dst_ref=block(target, me),
                send_sem=send_sem.at[number],
                recv_sem=recv_sem.at[number],
                device_id=(tx, ty),
                device_id_type=MESH,
            ).start()

    def wait_bytes(ref, sem):
        pltpu.make_async_copy(ref, ref, sem).wait()

    loads[2].wait()
    a = [atm_ref[i : i + 1, :] for i in range(6)]
    speed = jnp.sqrt(a[0] * a[0] + a[1] * a[1] + 0.25)
    rows4 = [
        0.5 * speed * (a[2] - a[5]),
        a[4] - 0.3 * speed * a[3],
        0.2 * speed * a[0],
        0.2 * speed * a[1],
    ]
    blank = jnp.zeros((12, 128), F32)
    for b in range(48):
        flux[b] = jnp.concatenate(
            [v[:, b * 128 : b * 128 + 128] for v in rows4] + [blank], axis=0
        ).astype(BF16)

    loads[0].wait()
    loads[1].wait()
    hit = (iota((128, 256), 0) == owner_ref[...]).astype(F32)
    before = (iota((256, 256), 0) < iota((256, 256), 1)).astype(BF16)
    rank = dot(hit.astype(BF16), before)
    perm = [jnp.where(rank == float(r), hit, 0.0) for r in range(4)]
    rows_f = row_ref[...].astype(F32) + 1.0
    lane128 = iota((128, 128), 1)
    row_msg = jnp.zeros((128, 128), F32)
    for r in range(4):
        at = jnp.sum(perm[r] * rows_f, axis=1, keepdims=True) - 1.0
        row_msg = jnp.where(lane128 == r, at, row_msg)
        perm_t[:, r * 128 : r * 128 + 128] = jnp.transpose(perm[r]).astype(BF16)
    row_held[...] = row_msg
    for t in range(8):
        row_out[t] = row_held[pl.ds(t, 16, stride=8), :]

    loads[7].wait()
    loads[8].wait()
    wet = wet_ref[...].astype(F32)
    kappa = kappa_ref[...]
    row8 = iota((8, 128), 0)
    for side, r in ((0, 0), (1, 63)):
        coef_x[side] = jnp.where(row8 == 0, kappa[r : r + 1, :], wet[r : r + 1, :])
    lane = iota((64, 128), 1)
    low, high = lane == 0, lane == 127
    packed = jnp.where(low, pltpu.roll(kappa, 1, 1), pltpu.roll(wet, 2, 1))
    packed = jnp.where(lane == 2, pltpu.roll(kappa, 2, 1), packed)
    coef_y[...] = jnp.where(lane == 3, pltpu.roll(wet, 3, 1), packed)

    for i in (3, 4, 5):
        loads[i].wait()

    def forward(g, _):
        for i in range(16):
            p = g * 16 + i
            out = dot(flux[block_s[0, p]], weights[tile_s[0, p]])
            contrib[pl.ds(pl.multiple_of(p * 8, 8), 8), :] = out[0:8]
        return 0

    lax.fori_loop(0, 1, forward, 0)

    pl.semaphore_wait(barrier, 22)
    for r in range(1, 8):
        pl.semaphore_signal(ready, inc=1, device_id=(gx, (gy + r) % 8), device_id_type=MESH)
    pltpu.make_async_copy(row_out.at[gy], row_mid.at[gy], row_rs.at[0]).start()
    for r in range(1, 8):
        t = (gy + r) % 8
        pltpu.make_async_remote_copy(
            src_ref=row_out.at[t],
            dst_ref=row_mid.at[gy],
            send_sem=row_ss.at[0],
            recv_sem=row_rs.at[0],
            device_id=(gx, t),
            device_id_type=MESH,
        ).start()

    lax.fori_loop(1, 16, forward, 0)

    part_h, part_l = split(
        jnp.concatenate([contrib[pl.ds(c, 256, stride=8), :] for c in range(4)], axis=1)
    )
    for r in range(4):
        pick = perm[r].astype(BF16)
        out = dot(pick, part_h) + dot(pick, part_l)
        for c in range(4):
            send_f[pl.ds(c * 4 + r, 128, stride=16), :] = out[:, c * 128 : c * 128 + 128]

    wait_bytes(row_mid, row_rs.at[0])
    mid = row_mid[...].reshape(128, 128)
    row_held[...] = mid
    for t in range(16):
        row_next[t] = row_held[pl.ds(t, 8, stride=16), :]
    pltpu.make_async_copy(row_next.at[gx], row_in.at[gx], row_rs.at[1]).start()
    for r in range(1, 16):
        t = (gx + r) % 16
        pltpu.make_async_remote_copy(
            src_ref=row_next.at[t],
            dst_ref=row_in.at[gx],
            send_sem=row_ss.at[1],
            recv_sem=row_rs.at[1],
            device_id=(t, gy),
            device_id_type=MESH,
        ).start()

    near = [((gx + 15) % 16, gy), ((gx + 1) % 16, gy), (gx, (gy + 7) % 8), (gx, (gy + 1) % 8)]

    def swap(number, sources, targets):
        copies = []
        for side in range(4):
            copies.append(
                pltpu.make_async_remote_copy(
                    src_ref=sources[side],
                    dst_ref=targets[side ^ 1],
                    send_sem=halo_ss.at[number, side],
                    recv_sem=halo_rs.at[number, side ^ 1],
                    device_id=near[side],
                    device_id_type=MESH,
                )
            )
        for copy in copies:
            copy.start()
        return copies

    pl.semaphore_wait(ready, 7)
    send_all(0, send_f, recv_f, 16, 16, ORDER, True)
    coef_copies = swap(
        0,
        [coef_x.at[0], coef_x.at[1], coef_y, coef_y],
        [coef_hx.at[0], coef_hx.at[1], coef_hy.at[0], coef_hy.at[1]],
    )

    wait_bytes(row_in, row_rs.at[1])
    rows_in = row_in[...].reshape(128, 128)
    rows_t = jnp.transpose(rows_in)
    x64 = iota((64, 128), 0).astype(F32)
    place = jnp.concatenate([(x64 == rows_t[r : r + 1, :]).astype(F32) for r in range(4)], axis=1)
    place = place.astype(BF16)
    twice = (lane128 % 64).astype(F32)
    fetch = [(rows_in[:, r : r + 1] == twice).astype(F32).astype(BF16) for r in range(4)]

    def give_back(source, target, pitch):
        parts = [split(v) for v in source]
        stacked = jnp.concatenate([jnp.concatenate([h, l], axis=0) for h, l in parts], axis=1)
        for r in range(4):
            out = dot(fetch[r], stacked)
            for c in range(len(source)):
                target[pl.ds(c * 4 + r, 128, stride=pitch), :] = out[:, c * 128 : c * 128 + 128]

    give_back([wet], send_w, 8)
    send_all(1, send_w, recv_w, 8, 4, ORDER, True)

    loads[9].wait()
    loads[10].wait()

    def solve(i, _):
        def at(level):
            return pl.ds(pl.multiple_of(level * 64 + i * 8, 8), 8)

        kap = [vert[at(l), :] for l in range(16)]
        face = [0.5 * (kap[l] + kap[l + 1]) for l in range(15)]
        inv, upper = [], []
        for l in range(16):
            above = face[l - 1] if l > 0 else 0.0
            below = face[l] if l < 15 else 0.0
            diagonal = 1.0 + above + below
            inv.append(1.0 / (diagonal + above * upper[-1] if l > 0 else diagonal))
            upper.append(-below * inv[-1])
        for field in range(5):
            held = []
            for l in range(16):
                if field < 4:
                    value = planes[at(field * 16 + l), :]
                    value = value + face[l - 1] * held[-1] if l > 0 else value
                    held.append(value * inv[l])
                else:
                    held.append(face[l - 1] * held[-1] * inv[l] if l > 0 else inv[l])
            value = held[15]
            for l in range(15, -1, -1):
                value = held[l] - upper[l] * value if l < 15 else value
                if field < 4:
                    planes[at(field * 16 + l), :] = value
                else:
                    gain[at(l), :] = value
        return 0

    lax.fori_loop(0, 8, solve, 0)

    for copy in coef_copies:
        copy.wait()

    def edge_row(side, row, there):
        return jnp.where(there, coef_hx[side, row : row + 1, :], 0.0)

    row64 = iota((64, 128), 0)
    sides = []
    for side, shift, there, edge in (
        (0, 1, gx > 0, row64 == 0),
        (1, 63, gx < 15, row64 == 63),
    ):
        sides.append(
            [
                jnp.where(edge, edge_row(side, v, there), pltpu.roll(field, shift, 0))
                for v, field in enumerate((kappa, wet))
            ]
        )
    for side, shift, there, edge, lanes in (
        (0, 1, gy > 0, low, (0, 1)),
        (1, 127, gy < 7, high, (2, 3)),
    ):
        got = jnp.where(there, coef_hy[side], 0.0)
        goal = 0 if side == 0 else 127
        sides.append(
            [
                jnp.where(edge, pltpu.roll(got, (goal - lanes[v]) % 128, 1), pltpu.roll(field, shift, 1))
                for v, field in enumerate((kappa, wet))
            ]
        )
    for n, (kappa_n, wet_n) in enumerate(sides):
        faces[n] = 0.25 * (kappa + kappa_n) * wet * wet_n

    wait_bytes(recv_f, recv_sem.at[0])
    for c in range(4):
        got = jnp.concatenate(
            [recv_f[pl.ds(c * 4 + r, 128, stride=16), :] for r in range(4)], axis=0
        )
        got_h, got_l = split(got)
        forcing[c] = (dot(place, got_h) + dot(place, got_l)) * wet

    def mix_tracers(l, _):
        response = gain[pl.ds(pl.multiple_of(l * 64, 64), 64), :]
        for c in range(2):
            at = pl.ds(pl.multiple_of(c * 1024 + l * 64, 64), 64)
            planes[at, :] = planes[at, :] + response * forcing[c]
        return 0

    lax.fori_loop(0, 16, mix_tracers, 0)

    pair = lane // 2

    def send_edges(number, source):
        edge_x[number, 0] = source[pl.ds(0, 32, stride=64), :]
        edge_x[number, 1] = source[pl.ds(63, 32, stride=64), :]

        def pack(k, held):
            plane = source[pl.ds(pl.multiple_of(k * 64, 64), 64), :]
            return jnp.where(pair == k, pltpu.roll(plane, 2 * k + 1, 1), held)

        edge_y[number] = lax.fori_loop(0, 32, pack, jnp.zeros((64, 128), F32), unroll=8)
        return swap(
            1 + number,
            [edge_x.at[number, 0], edge_x.at[number, 1], edge_y.at[number], edge_y.at[number]],
            [halo_x.at[number, 0], halo_x.at[number, 1], halo_y.at[number, 0], halo_y.at[number, 1]],
        )

    def join_sides(number):
        left, right = halo_y[number, 0], halo_y[number, 1]
        sides_y[number] = jnp.where(lane % 2 == 1, pltpu.roll(left, 1, 1), pltpu.roll(right, 127, 1))

    def diffuse(number, source, target, k):
        at = pl.ds(pl.multiple_of(k * 64, 64), 64)
        q = source[at, :]
        up = jnp.where(row64 == 0, halo_x[number, 0, pl.ds(k, 1), :], pltpu.roll(q, 1, 0))
        down = jnp.where(row64 == 63, halo_x[number, 1, pl.ds(k, 1), :], pltpu.roll(q, 63, 0))
        beside = pltpu.roll(sides_y[number], 127 - 2 * k, 1)
        left = jnp.where(low, beside, pltpu.roll(q, 1, 1))
        right = jnp.where(high, beside, pltpu.roll(q, 127, 1))
        total = q
        for n, other in enumerate((up, down, left, right)):
            total = total + faces[n] * (other - q)
        target[at, :] = total

    copies_1 = send_edges(0, planes)
    response = gain[0:64, :]
    give_back(
        [(planes[c * 1024 : c * 1024 + 64, :] + response * forcing[c]) * wet for c in (2, 3)],
        send_1,
        8,
    )
    send_all(2, send_1, recv_1, 8, 8, ORDER[:64], True)
    for copy in copies_1:
        copy.wait()
    join_sides(0)

    def pass_1(k, _):
        diffuse(0, planes, first, k)
        return 0

    lax.fori_loop(0, 32, pass_1, 0, unroll=4)
    copies_2 = send_edges(1, first)
    send_all(2, send_1, recv_1, 8, 8, ORDER[64:], False)
    for copy in copies_2:
        copy.wait()
    join_sides(1)
    diffuse(1, first, planes, 0)
    diffuse(1, first, planes, 16)
    give_back([planes[c * 1024 : c * 1024 + 64, :] * wet for c in (0, 1)], send_2, 8)
    send_all(3, send_2, recv_2, 8, 8, ORDER, True)

    def turn(t, _):
        weights_t[t] = jnp.transpose(weights[t])
        return 0

    lax.fori_loop(0, 128, turn, 0, unroll=8)

    def pass_2(l, _):
        diffuse(1, first, planes, l)
        diffuse(1, first, planes, l + 16)
        return 0

    lax.fori_loop(1, 16, pass_2, 0, unroll=3)

    def mix_flow(l, _):
        response = gain[pl.ds(pl.multiple_of(l * 64, 64), 64), :]
        for c in (2, 3):
            at = pl.ds(pl.multiple_of(c * 1024 + l * 64, 64), 64)
            planes[at, :] = planes[at, :] + response * forcing[c]
        return 0

    lax.fori_loop(0, 16, mix_flow, 0)
    store = pltpu.make_async_copy(planes, ocean_out, out_sem.at[0])
    store.start()


    def take(source, pitch, c, plane):
        got = jnp.concatenate(
            [source[pl.ds(c * 4 + r, 128, stride=pitch), :] for r in range(4)], axis=0
        )
        for half, part in enumerate(split(got)):
            picks[pl.ds(half * 8 + plane, 256, stride=16), :] = dot(perm_t[...], part)

    wait_bytes(recv_w.at[pl.ds(0, 512), :], recv_sem.at[1])
    take(recv_w, 8, 0, 4)
    wait_bytes(recv_1, recv_sem.at[2])
    for c in range(2):
        take(recv_1, 8, c, c + 2)
    wait_bytes(recv_2, recv_sem.at[3])
    for c in range(2):
        take(recv_2, 8, c, c)

    def backward(g, _):
        for i in range(32):
            p = g * 32 + i
            rows = picks[pl.ds(pl.multiple_of(p * 16, 16), 16), :].astype(BF16)
            out = dot(rows, weights_t[tile_s[0, p]])
            back[pl.ds(pl.multiple_of(p * 8, 8), 8), :] = out[0:8] + out[8:16]
        return 0

    lax.fori_loop(0, 8, backward, 0)

    loads[6].wait()
    of_block = iota((192, 256), 0) // 4 == block_ref[...]
    plane_of = iota((192, 256), 0) % 4
    num = jnp.zeros((192, 128), F32)
    for c in range(4):
        member = jnp.where(of_block & (plane_of == c), 1.0, 0.0).astype(BF16)
        for part in split(back[pl.ds(c, 256, stride=8), :]):
            num = num + dot(member, part)
    den = jnp.zeros((192, 128), F32)
    member = jnp.where(of_block, 1.0, 0.0).astype(BF16)
    for part in split(back[pl.ds(4, 256, stride=8), :]):
        den = den + dot(member, part)
    atm_held[...] = num / jnp.maximum(den, 0.1)
    store_atm = pltpu.make_async_copy(atm_held, atm_out, out_sem.at[1])
    store_atm.start()

    wait_bytes(send_f.at[pl.ds(0, 127 * 16), :], send_sem.at[0])
    wait_bytes(row_out.at[pl.ds(0, 7)], row_ss.at[0])
    wait_bytes(row_next.at[pl.ds(0, 15)], row_ss.at[1])
    wait_bytes(send_w.at[pl.ds(0, 127 * 4), :], send_sem.at[1])
    wait_bytes(send_1.at[pl.ds(0, 127 * 8), :], send_sem.at[2])
    wait_bytes(send_2.at[pl.ds(0, 127 * 8), :], send_sem.at[3])
    store.wait()
    store_atm.wait()


def hand_over(ocean_in, atm_in, ocean_out, atm_out, held, atm_held, atm_done, in_sem, out_sem):
    atm_load = pltpu.make_async_copy(atm_in, atm_held, in_sem.at[4])
    atm_load.start()
    parts = [pl.ds(i * 1024, 1024) for i in range(4)]
    loads = [
        pltpu.make_async_copy(ocean_in.at[at, :], held.at[at, :], in_sem.at[i])
        for i, at in enumerate(parts)
    ]
    stores = [
        pltpu.make_async_copy(held.at[at, :], ocean_out.at[at, :], out_sem.at[i])
        for i, at in enumerate(parts)
    ]
    stores.append(pltpu.make_async_copy(atm_done, atm_out, out_sem.at[4]))
    for copy in loads:
        copy.start()
    atm_load.wait()
    for b in range(48):
        atm_done[:, b * 128 : b * 128 + 128] = atm_held[b * 4 : b * 4 + 4, :]
    stores[4].start()
    for load, store in zip(loads, stores):
        load.wait()
        store.start()
    for copy in stores:
        copy.wait()


def local(
    atm_state,
    pair_block,
    pair_owner,
    pair_row,
    pair_tile,
    remap_weight,
    wet_mask,
    ocean_state,
    vert_kappa,
    horiz_kappa,
):
    hbm = pl.BlockSpec(memory_space=pl.ANY)
    dma = pltpu.SemaphoreType.DMA

    def buffer(*shape, dtype=F32):
        return pltpu.VMEM(shape, dtype)

    ocean, atm = pl.pallas_call(
        kernel,
        out_shape=(
            jax.ShapeDtypeStruct((4096, 128), F32),
            jax.ShapeDtypeStruct((192, 128), F32),
        ),
        in_specs=[hbm] * 10,
        out_specs=(hbm, hbm),
        scratch_shapes=[
            pltpu.SMEM((1, 256), jnp.int32),
            pltpu.SMEM((1, 256), jnp.int32),
            buffer(1, 256, dtype=jnp.int32),
            buffer(1, 256, dtype=jnp.int32),
            buffer(1, 256, dtype=jnp.int32),
            buffer(6, 6144),
            buffer(64, 128, dtype=jnp.int32),
            buffer(64, 128),
            buffer(192, 128),
            buffer(128, 128, 128, dtype=BF16),
            buffer(128, 128, 128, dtype=BF16),
            buffer(4096, 128),
            buffer(1024, 128),
            buffer(1024, 128),
            buffer(2048, 128),
            buffer(48, 16, 128, dtype=BF16),
            buffer(2048, 128),
            buffer(256, 512, dtype=BF16),
            buffer(128, 128),
            buffer(8, 16, 128),
            buffer(8, 16, 128),
            buffer(16, 8, 128),
            buffer(16, 8, 128),
            buffer(2048, 128),
            buffer(2048, 128),
            buffer(1024, 128),
            buffer(1024, 128),
            buffer(1024, 128),
            buffer(1024, 128),
            buffer(1024, 128),
            buffer(1024, 128),
            buffer(4, 64, 128),
            buffer(4, 64, 128),
            buffer(2, 2, 32, 128),
            buffer(2, 2, 32, 128),
            buffer(2, 64, 128),
            buffer(2, 2, 64, 128),
            buffer(2, 64, 128),
            buffer(2, 8, 128),
            buffer(2, 8, 128),
            buffer(64, 128),
            buffer(2, 64, 128),
            buffer(4096, 128),
            buffer(2048, 128),
            dma((11,)),
            dma((2,)),
            dma((4,)),
            dma((4,)),
            dma((3, 4)),
            dma((3, 4)),
            dma((2,)),
            dma((2,)),
            pltpu.SemaphoreType.REGULAR,
        ],
        compiler_params=pltpu.CompilerParams(
            collective_id=0, has_side_effects=True, vmem_limit_bytes=63 << 20
        ),
        name="couple",
    )(
        pair_tile.reshape(1, 256),
        pair_block.reshape(1, 256),
        pair_owner.reshape(1, 256),
        pair_row.reshape(1, 256),
        atm_state,
        wet_mask,
        horiz_kappa,
        remap_weight,
        ocean_state.reshape(4096, 128),
        vert_kappa.reshape(1024, 128),
    )
    ocean_next, atm_surface = pl.pallas_call(
        hand_over,
        out_shape=(
            jax.ShapeDtypeStruct((4096, 128), F32),
            jax.ShapeDtypeStruct((4, 6144), F32),
        ),
        in_specs=[hbm, hbm],
        out_specs=(hbm, hbm),
        scratch_shapes=[
            buffer(4096, 128),
            buffer(192, 128),
            buffer(4, 6144),
            dma((5,)),
            dma((5,)),
        ],
        compiler_params=pltpu.CompilerParams(vmem_limit_bytes=63 << 20),
        name="hand_over",
    )(ocean, atm)
    return (ocean_next.reshape(4, 16, 64, 128), atm_surface)


def solution(mesh):
    placed = (
        P(None, ("gx", "gy")),
        P(("gx", "gy")),
        P(("gx", "gy"), None),
        P(("gx", "gy")),
        P(("gx", "gy")),
        P(("gx", "gy"), None, None),
        P("gx", "gy"),
        P(None, None, "gx", "gy"),
        P(None, "gx", "gy"),
        P("gx", "gy"),
    )
    return jax.shard_map(
        local,
        mesh=mesh,
        in_specs=placed,
        out_specs=(P(None, None, "gx", "gy"), P(None, ("gx", "gy"))),
        check_vma=False,
    )
```
